256 devices in a mesh: tok: 16 (over z, core), exp: 16 (over y, x).
Axes of the slice: x: 4, y: 4, z: 8, core: 2. Of those that a mesh axis runs over, the one named last changes fastest.
Arguments:
- tokens: bfloat16 [131072, 2048], P(('tok', 'exp')), may hold values from -40 to 40
- first_factor: bfloat16 [128, 2048, 256], P('exp'), may hold values from -0.125 to 0.125
- expert_ids: int32 [131072, 8], P(('tok', 'exp')), may hold values from 0 to 127, all different within a row; in each aligned block of 512 rows (0 to 511, 512 to 1023, ...) at most 40 rows name the same one
Outputs:
- codes: bfloat16 [131072, 8, 256], P(('tok', 'exp'))
- upper_factor: float32 [128, 256, 256], P('exp')
The draws below stay inside these ranges and needn't reach their ends.
Inputs may be any that keep to these rules, and one draw needn't show every extreme that they name: `expert_ids`: within the rows of one device (aligned blocks of 512 tokens) no expert is named more than 40 times, a bound that some block reaches; each token names 8 different experts, and every expert is named by some token.
All inputs are finite; a program needn't handle non-finite values.
Results may differ from the reference program's by a relative error of at most 0.0058.
Values may be sent and summed in bfloat16 or wider, within the bound.
No kernel may reach another device: no remote copies, remote signals or barrier semaphores. Data moves between devices by JAX's collectives and lax.ppermute only.
A program may use at most 256 MiB of HBM per device.

```python
import math
import jax
import jax.numpy as jnp
import numpy as np
from jax import lax

D = 2048
K = 256
TOP = 8
TOK_DEV = 512
EXPERTS = 128
TOKENS = 131072
MOST = 40


def draw_tokens(key, part):
    key = jax.random.fold_in(key, 11)
    key_values, key_scales = jax.random.split(key, 2)
    row_trend = 3.0 ** (jnp.arange(TOKENS, dtype=jnp.float32) / (TOKENS - 1))
    row_jitter = jnp.exp(jax.random.uniform(key_scales, (TOKENS, 1), jnp.float32, 0.0, math.log(3.4)))
    values = jax.random.normal(key_values, (TOKENS, D), jnp.float32)
    return jnp.clip(values * row_trend[:, None] * row_jitter, -40.0, 40.0).astype(jnp.bfloat16)


def levels(own_key, extent, pieces, least, largest):
    loudness = 1.0
    for dim, shards_of in pieces:
        steps = jax.random.uniform(jax.random.fold_in(jax.random.fold_in(own_key, 6), dim), (shards_of,), jnp.float32, least / len(pieces), largest / len(pieces))
        loudness = loudness * jnp.repeat(jnp.exp(steps), extent[dim] // shards_of).reshape((-1,) + (1,) * (len(extent) - 1 - dim))
    return loudness


def assign_block(stream_key, own, number, rows, count, top, limit, lean):
    sequence = jax.random.permutation(stream_key, count)
    crowded, common = portions_of(count, rows * top, limit, lean, True), portions_of(count, rows * top, limit, lean, False)
    places = jnp.arange(count)

    def named(sizes, turn):
        used = int((sizes > 0).sum())
        fixed = max(1, used // 4)
        passed = fixed + (places - fixed + turn * (used - fixed)) % max(1, count - fixed)
        return jnp.zeros((count,), jnp.int32).at[sequence[jnp.where(places < fixed, places, passed)]].set(jnp.asarray(sizes, jnp.int32))

    sizes = jnp.where(number % 4 == 0, named(crowded, number // 4), named(common, number - number // 4 - 1))
    mixed = jax.random.permutation(jax.random.fold_in(own, 3), count)
    source_of, sink = mixed[0:count // 2 * 2:2], mixed[1:count // 2 * 2:2]
    slack = jnp.minimum(sizes[source_of] - 1, limit - sizes[sink]) // 2
    slack = jnp.where((source_of == sequence[0]) | (sink == sequence[0]) | (sizes[sink] == 0), 0, jnp.maximum(slack, 0))
    passed = jax.random.randint(jax.random.fold_in(own, 4), (count // 2,), 0, 1 << 20) % (slack + 1)
    sizes = sizes.at[source_of].add(-passed).at[sink].add(passed)
    members = jnp.searchsorted(jnp.cumsum(sizes), jnp.arange(rows * top), side="right").astype(jnp.int32)
    table = members.reshape(top, rows).T
    table = table[jax.random.permutation(jax.random.fold_in(own, 1), rows)]
    turn = jax.random.randint(jax.random.fold_in(own, 2), (rows, 1), 0, top)
    return jnp.take_along_axis(table, (jnp.arange(top)[None, :] + turn) % top, axis=1)


def portions_of(number_of, total, most, slope, full):
    weights = [(1 << 20) // math.isqrt(rank ** slope) + 1 for rank in range(1, number_of + 1)]
    largest = most if full else min(most, max(-(-total // number_of), total * weights[0] // sum(weights)))
    least = 1 if total - largest >= number_of - 1 else 0
    given, spare = [largest] + [least] * (number_of - 1), total - largest - least * (number_of - 1)
    while spare > 0:
        movable = [i for i in range(1, number_of) if given[i] < largest] or [i for i in range(1, number_of) if given[i] < most]
        pool, left = sum([weights[i] for i in movable]), spare
        for i in movable:
            extra = min(most - given[i], max(1, left * weights[i] // pool), spare)
            given[i] = given[i] + extra
            spare = spare - extra
    return np.array(given)


def normal_values(rng, extent, spread, limit, pieces=(), kind=jnp.bfloat16):
    values = jax.random.normal(rng, extent, jnp.float32) * spread
    if len(pieces) > 0:
        values = levels(rng, extent, pieces, -0.22, 0.18) * values
    return jnp.clip(values, min=-limit, max=limit).astype(kind)


def setup_inputs(seed: int = 0) -> dict:
    seeds = jax.random.split(jax.random.key(seed), 4)
    tokens = draw_tokens(jax.random.fold_in(seeds[3], 71), 0)
    first_factor = normal_values(seeds[1], (EXPERTS, D, K), D ** -0.5, 0.125, ((0, 16),))
    expert_ids_keys = jax.random.split(jax.random.fold_in(seeds[2], 1), TOKENS // TOK_DEV)
    expert_ids_turns = jax.random.permutation(jax.random.fold_in(seeds[2], 3), TOKENS // TOK_DEV)
    expert_ids = jax.vmap(lambda own, number: assign_block(jax.random.fold_in(seeds[2], 2), own, number, TOK_DEV, EXPERTS, TOP, MOST, 1))(expert_ids_keys, expert_ids_turns).reshape((TOKENS, TOP))
    return dict(tokens=tokens, first_factor=first_factor, expert_ids=expert_ids)


RIDGE = 0.1

def reference(tokens, first_factor, expert_ids):
    pair_expert = expert_ids.reshape(-1).astype(jnp.int32)
    pair_count = pair_expert.shape[0]
    capacity = TOKENS // TOK_DEV * MOST
    sort_order = jnp.argsort(pair_expert, stable=True).astype(jnp.int32)
    counts = jax.ops.segment_sum(jnp.ones((pair_count,), jnp.int32), pair_expert, EXPERTS)
    offsets = (jnp.cumsum(counts) - counts).astype(jnp.int32)
    order_padded = jnp.concatenate([sort_order, jnp.zeros((capacity,), jnp.int32)])
    gram_scale = EXPERTS / (TOP * TOKENS)

    def one_expert(expert):
        pair_index = lax.dynamic_slice_in_dim(order_padded, offsets[expert], capacity)
        live_rows = jnp.arange(capacity, dtype=jnp.int32) < counts[expert]
        row_block = jnp.where(live_rows[:, None], tokens[pair_index // TOP], jnp.zeros((), tokens.dtype))
        projected = jnp.dot(row_block.astype(jnp.float32), first_factor[expert].astype(jnp.float32), preferred_element_type=jnp.float32).astype(jnp.bfloat16)
        gram_matrix = gram_scale * jnp.dot(projected.T.astype(jnp.float32), projected.astype(jnp.float32), preferred_element_type=jnp.float32)
        gram_matrix = gram_matrix + RIDGE * jnp.eye(K, dtype=jnp.float32)
        lower_factor = jnp.linalg.cholesky(gram_matrix)
        code_rows = jax.scipy.linalg.solve_triangular(lower_factor, projected.astype(jnp.float32).T, lower=True).T
        return (lower_factor.T, code_rows.astype(jnp.bfloat16))
    upper_factors, codes_sorted = lax.map(one_expert, jnp.arange(EXPERTS, dtype=jnp.int32))
    position = jnp.zeros((pair_count,), jnp.int32).at[sort_order].set(jnp.arange(pair_count, dtype=jnp.int32))
    sorted_rank = position - offsets[pair_expert]
    codes = codes_sorted[pair_expert, sorted_rank].reshape(TOKENS, TOP, K)
    return (codes, upper_factors)
```

```python
import functools

import jax
import jax.numpy as jnp
from jax import lax
from jax.experimental import pallas as pl
from jax.experimental.pallas import tpu as pltpu
from jax.sharding import Mesh
from jax.sharding import PartitionSpec as P

RIDGE = 0.1
BLOCK = 32
VMEM_BYTES = 48 * 2**20


def exact_dot(a, b, dims):
    return lax.dot_general(
        a, b, (dims, ((), ())), precision=lax.Precision.HIGHEST, preferred_element_type=jnp.float32
    )


def factor_kernel(gram_ref, upper_ref, high_ref, low_ref, work, *, block):
    experts, _, half, _ = gram_ref.shape
    size = 2 * half
    lanes = 128
    groups = lanes // block
    tiles = experts // groups
    rows_h = lax.broadcasted_iota(jnp.int32, (half, half), 0)
    cols_h = lax.broadcasted_iota(jnp.int32, (half, half), 1)
    ridge_h = jnp.where(rows_h == cols_h, RIDGE, 0.0).astype(jnp.float32)
    for e in range(experts):
        work[e, :half, :half] = gram_ref[e, 0] + ridge_h
        work[e, :half, half:] = gram_ref[e, 1]
        work[e, half:, half:] = gram_ref[e, 2] + ridge_h
    lane = lax.broadcasted_iota(jnp.int32, (block, lanes), 1)
    row = lax.broadcasted_iota(jnp.int32, (block, lanes), 0)
    unit = jnp.where(lane % block == row, 1.0, 0.0).astype(jnp.float32)
    base = (lane // block) * block
    for k in range(size // block):
        lo, hi = k * block, (k + 1) * block
        packed = [
            jnp.concatenate([work[t * groups + g, lo:hi, lo:hi] for g in range(groups)], axis=1)
            for t in range(tiles)
        ]
        inverse = [unit for _ in range(tiles)]
        scales = [jnp.ones((block, lanes), jnp.float32) for _ in range(tiles)]
        for j in range(block):
            for t in range(tiles):
                s, n = packed[t], inverse[t]
                column = jnp.take_along_axis(s, base + j, axis=1, mode="promise_in_bounds")
                pivot = column[j : j + 1, :]
                scales[t] = jnp.where(row == j, lax.rsqrt(pivot), scales[t])
                factor = jnp.where(row > j, column * (1.0 / pivot), 0.0)
                packed[t] = s - factor * s[j : j + 1, :]
                inverse[t] = n - factor * n[j : j + 1, :]
        packed = [jnp.where(lane % block >= row, s * c, 0.0) for s, c in zip(packed, scales)]
        inverse = [n * c for n, c in zip(inverse, scales)]
        for e in range(experts):
            t, g = e // groups, e % groups
            work[e, lo:hi, lo:hi] = jnp.eye(block, dtype=jnp.float32)
            strip = exact_dot(
                inverse[t][:, g * block : (g + 1) * block], work[e, lo:hi, :], ((1,), (0,))
            )
            if lo:
                upper_ref[e, lo:hi, :lo] = jnp.zeros((block, lo), jnp.float32)
            upper_ref[e, lo:hi, lo:hi] = packed[t][:, g * block : (g + 1) * block]
            work[e, lo:hi, :] = strip
            if hi < size:
                upper_ref[e, lo:hi, hi:] = strip[:, hi:]
                work[e, hi:, lo:hi] = jnp.zeros((size - hi, block), jnp.float32)
                work[e, hi:, :] = work[e, hi:, :] - exact_dot(strip[:, hi:], strip, ((0,), (0,)))
    rows = lax.broadcasted_iota(jnp.int32, (size, size), 0)
    cols = lax.broadcasted_iota(jnp.int32, (size, size), 1)
    for e in range(experts):
        whole = jnp.where(rows >= cols, work[e], 0.0)
        high = whole.astype(jnp.bfloat16)
        high_ref[e] = high
        low_ref[e] = (whole - high.astype(jnp.float32)).astype(jnp.bfloat16)


def factorize(gram_blocks):
    experts, _, half, _ = gram_blocks.shape
    size = 2 * half
    square = (experts, size, size)
    return pl.pallas_call(
        functools.partial(factor_kernel, block=BLOCK),
        out_shape=(
            jax.ShapeDtypeStruct(square, jnp.float32),
            jax.ShapeDtypeStruct(square, jnp.bfloat16),
            jax.ShapeDtypeStruct(square, jnp.bfloat16),
        ),
        scratch_shapes=[pltpu.VMEM(square, jnp.float32)],
        compiler_params=pltpu.CompilerParams(vmem_limit_bytes=VMEM_BYTES),
        name="factorize",
    )(gram_blocks)


def slot_ranks(ids, experts):
    rows = ids.shape[0]
    named = (ids[:, :, None] == jnp.arange(experts, dtype=jnp.int32)).any(axis=1)
    earlier = jnp.arange(rows)[:, None] > jnp.arange(rows)[None, :]
    rank = jnp.dot(
        earlier.astype(jnp.bfloat16), named.astype(jnp.bfloat16), preferred_element_type=jnp.float32
    )
    return jnp.where(named, rank, -1.0).astype(jnp.int32)


def reduce_gram(partial_gram):
    experts, parts, half, _ = partial_gram.shape
    cores, layers = lax.axis_size("c"), lax.axis_size("z")
    core = lax.axis_index("c")
    split = partial_gram.reshape(cores, -1, half)
    swap = [(i, (i + 1) % cores) for i in range(cores)]
    mine = lax.dynamic_index_in_dim(split, core, 0, keepdims=False)
    other = lax.dynamic_index_in_dim(split, 1 - core, 0, keepdims=False)
    mine = mine + lax.ppermute(other, "c", swap)
    pieces = lax.all_to_all(mine.reshape(layers, -1, half), "z", 0, 0, tiled=True)
    mine = lax.all_gather(jnp.sum(pieces, axis=0), "z", tiled=True)
    other = lax.ppermute(mine, "c", swap)
    whole = jnp.where(core == 0, jnp.stack([mine, other]), jnp.stack([other, mine]))
    return whole.reshape(experts, parts, half, half)


def local(tokens, first_factor, expert_ids):
    groups = lax.axis_size(("y", "x"))
    tok_ranks = lax.axis_size(("z", "c"))
    per_group, model_dim, rank_k = first_factor.shape
    tok_rows, top_k = expert_ids.shape
    experts = groups * per_group
    capacity = tok_rows * top_k * 5 // (4 * experts)
    gram_scale = experts / (top_k * tok_rows * tok_ranks * groups)
    half = rank_k // 2
    ranks = slot_ranks(expert_ids, experts)
    select = ranks.T[:, None, :] == jnp.arange(capacity, dtype=jnp.int32)[None, :, None]
    outgoing = jnp.einsum(
        "est,td->esd", select.astype(jnp.bfloat16), tokens, preferred_element_type=jnp.float32
    ).astype(jnp.bfloat16)
    incoming = lax.all_to_all(
        outgoing.reshape(groups, per_group, capacity, model_dim), ("y", "x"), 0, 0, tiled=True
    )
    projected = jnp.einsum(
        "slmd,ldk->slmk", incoming, first_factor, preferred_element_type=jnp.float32
    ).astype(jnp.bfloat16)
    partial_gram = gram_scale * jnp.einsum(
        "slmk,slmj->lkj", projected, projected, preferred_element_type=jnp.float32
    )
    partial_gram = jnp.stack(
        [
            partial_gram[:, :half, :half],
            partial_gram[:, :half, half:],
            partial_gram[:, half:, half:],
        ],
        axis=1,
    )
    upper, high, low = factorize(reduce_gram(partial_gram))
    codes = sum(
        jnp.einsum("slmk,ljk->slmj", projected, term, preferred_element_type=jnp.float32)
        for term in (high, low)
    ).astype(jnp.bfloat16)
    returned = lax.all_to_all(codes, ("y", "x"), 0, 0, tiled=True)
    own_rank = jnp.take_along_axis(ranks, expert_ids, axis=1)
    slot = (expert_ids * capacity + own_rank).reshape(-1)
    gathered = returned.reshape(experts * capacity, rank_k)[slot]
    return (gathered.reshape(tok_rows, top_k, rank_k), upper)


def solution(mesh):
    layers = mesh.shape["tok"] // 2
    side = 4
    fine = Mesh(
        mesh.devices.reshape(layers, 2, mesh.shape["exp"] // side, side), ("z", "c", "y", "x")
    )
    every = ("z", "c", "y", "x")
    in_specs = (P(every, None), P(("y", "x"), None, None), P(every, None))
    out_specs = (P(every, None, None), P(("y", "x"), None, None))
    return jax.shard_map(local, mesh=fine, in_specs=in_specs, out_specs=out_specs, check_vma=False)
```

```python
import functools

import jax
import jax.numpy as jnp
from jax import lax
from jax.experimental import pallas as pl
from jax.experimental.pallas import tpu as pltpu
from jax.sharding import Mesh
from jax.sharding import PartitionSpec as P

RIDGE = 0.1
BLOCK = 32
SIDE = 4
VMEM_BYTES = 48 * 2**20
NEAR = (0, -1, 1, 2)
WHOLE = pl.BlockSpec(memory_space=pltpu.VMEM)
SCALARS = pl.BlockSpec(memory_space=pltpu.SMEM)


def params():
    return pltpu.CompilerParams(vmem_limit_bytes=VMEM_BYTES)


def exact_dot(a, b, dims):
    return lax.dot_general(
        a, b, (dims, ((), ())), precision=lax.Precision.HIGHEST, preferred_element_type=jnp.float32
    )


def dot(a, b):
    return jnp.dot(a, b, preferred_element_type=jnp.float32)


def shift(array, axis, step):
    size = lax.axis_size(axis)
    return lax.ppermute(array, axis, [(i, (i + step) % size) for i in range(size)])


def select_kernel(rank_ref, first_ref, *rest, capacity):
    *second_refs, out_ref, picks = rest
    experts, tok_rows = rank_ref.shape[1:]

    @pl.when(pl.program_id(0) == 0)
    def _():
        slots = lax.broadcasted_iota(jnp.int32, (capacity, tok_rows), 0).astype(jnp.float32)
        for source in range(2):
            for pair in range(experts // 2):
                both = [
                    jnp.where(rank_ref[source, e : e + 1, :] == slots, 1.0, 0.0)
                    for e in (2 * pair, 2 * pair + 1)
                ]
                picks[source, pair * 2 * capacity : (pair + 1) * 2 * capacity, :] = jnp.concatenate(
                    both, axis=0
                ).astype(jnp.bfloat16)

    blocks = (first_ref[...], jnp.concatenate([r[...] for r in second_refs], axis=0))
    step = 8
    for e in range(0, experts, step):
        rows = slice(e * capacity, (e + step) * capacity)
        found = [dot(picks[source, rows, :], blocks[source]) for source in range(2)]
        for i in range(step):
            own = slice(i * capacity, (i + 1) * capacity)
            out_ref[e + i] = jnp.concatenate([found[0][own], found[1][own]], axis=0).astype(
                out_ref.dtype
            )


def select(ranks, first, second, capacity, columns=512):
    _, experts, tok_rows = ranks.shape
    width = first.shape[1]
    columns = min(columns, width)
    return pl.pallas_call(
        functools.partial(select_kernel, capacity=capacity),
        grid=(width // columns,),
        in_specs=[pl.BlockSpec(ranks.shape, lambda i: (0, 0, 0))]
        + [pl.BlockSpec((a.shape[0], columns), lambda i: (0, i)) for a in (first, *second)],
        out_specs=pl.BlockSpec((experts, 2 * capacity, columns), lambda i: (0, 0, i)),
        out_shape=jax.ShapeDtypeStruct((experts, 2 * capacity, width), first.dtype),
        scratch_shapes=[pltpu.VMEM((2, experts * capacity, tok_rows), jnp.bfloat16)],
        compiler_params=params(),
        cost_estimate=pl.CostEstimate(
            flops=4 * experts * capacity * tok_rows * width, bytes_accessed=2**24, transcendentals=0
        ),
        name="select",
    )(ranks, first, *second)


def project_own_kernel(at_ref, near_ref, far_ref, factor_ref, out_ref):
    rows = jnp.concatenate([near_ref[0], far_ref[0]], axis=0)
    out_ref[0] = dot(rows, factor_ref[0]).astype(out_ref.dtype)


def project_kernel(at_ref, near_ref, far_ref, shared_ref, mine_ref, other_ref, out_ref):
    rows = jnp.concatenate([near_ref[0], far_ref[0]], axis=0)
    shared = shared_ref[...]
    shared = shared.reshape(-1, shared.shape[-1])
    depth = shared.shape[0]
    half = mine_ref.shape[1]
    low, high = rows[:, depth : depth + half], rows[:, depth + half :]
    first = at_ref[1] == 0
    total = dot(rows[:, :depth], shared)
    total += dot(jnp.where(first, low, high), mine_ref[0])
    total += dot(jnp.where(first, high, low), other_ref[0])
    out_ref[0] = total.astype(out_ref.dtype)


def project(at, near, far, factors, per_group, start, count, index=None):
    width = near.shape[2]
    rank_k = factors[0].shape[-1]
    row_spec = lambda rows: pl.BlockSpec(
        (1, rows, width), lambda i, at: (at[0] * per_group + start + i, 0, 0)
    )
    plain = lambda a: pl.BlockSpec((1,) + a.shape[1:], lambda i, at: (i, 0, 0))
    if index is None:
        kernel, specs = project_own_kernel, [plain(factors[0])]
    else:
        shared = factors[0]
        kernel = project_kernel
        specs = [
            pl.BlockSpec(
                (shared.shape[0], 1, 1) + shared.shape[3:],
                lambda i, at: (0, index, start + i, 0, 0),
            ),
            plain(factors[1]),
            plain(factors[2]),
        ]
    rows = near.shape[1] + far.shape[1]
    return pl.pallas_call(
        kernel,
        grid_spec=pltpu.PrefetchScalarGridSpec(
            num_scalar_prefetch=1,
            grid=(count,),
            in_specs=[row_spec(near.shape[1]), row_spec(far.shape[1])] + specs,
            out_specs=pl.BlockSpec((1, rows, rank_k), lambda i, at: (i, 0, 0)),
        ),
        out_shape=jax.ShapeDtypeStruct((count, rows, rank_k), near.dtype),
        compiler_params=params(),
        cost_estimate=pl.CostEstimate(
            flops=2 * count * rows * width * rank_k,
            bytes_accessed=2 * count * width * (rows + rank_k),
            transcendentals=0,
        ),
        name="project",
    )(at, near, far, *factors)


def gram_kernel(at_ref, *refs, scale):
    *row_refs, mine_ref, other_ref = refs
    count, _, half, _ = mine_ref.shape
    core = at_ref[2]
    for out_ref, turn in ((mine_ref, core), (other_ref, 1 - core)):
        for i in range(count):
            rows = jnp.concatenate([r[turn * count + i] for r in row_refs], axis=0)
            lower, upper = rows[:, :half], rows[:, half:]
            transposed = ((0,), (0,))
            pairs = ((lower, lower), (lower, upper), (upper, upper))
            for block, (a, b) in enumerate(pairs):
                out_ref[i, block] = scale * lax.dot_general(
                    a, b, (transposed, ((), ())), preferred_element_type=jnp.float32
                )


def partial_grams(at, rows, scale):
    experts, _, rank_k = rows[0].shape
    half = jax.ShapeDtypeStruct((experts // 2, 3, rank_k // 2, rank_k // 2), jnp.float32)
    return pl.pallas_call(
        functools.partial(gram_kernel, scale=scale),
        in_specs=[SCALARS] + [WHOLE] * len(rows),
        out_specs=(WHOLE, WHOLE),
        out_shape=(half, half),
        compiler_params=params(),
        name="grams",
    )(at, *rows)


def factor_kernel(at_ref, mine_ref, other_ref, *refs, block, capacity):
    *row_refs, upper_ref, codes_ref, work, high_ref, low_ref = refs
    count, _, half, _ = mine_ref.shape
    experts = 2 * count
    size = 2 * half
    lanes = 128
    groups = lanes // block
    tiles = experts // groups
    y, x, core = at_ref[0], at_ref[1], at_ref[2]
    expert = lambda e: core * count + e if e < count else (1 - core) * count + e - count
    rows_h = lax.broadcasted_iota(jnp.int32, (half, half), 0)
    cols_h = lax.broadcasted_iota(jnp.int32, (half, half), 1)
    ridge_h = jnp.where(rows_h == cols_h, RIDGE, 0.0).astype(jnp.float32)
    for e in range(experts):
        source, i = (mine_ref, e) if e < count else (other_ref, e - count)
        work[e, :half, :half] = source[i, 0] + ridge_h
        work[e, :half, half:] = source[i, 1]
        work[e, half:, half:] = source[i, 2] + ridge_h
    lane = lax.broadcasted_iota(jnp.int32, (block, lanes), 1)
    row = lax.broadcasted_iota(jnp.int32, (block, lanes), 0)
    unit = jnp.where(lane % block == row, 1.0, 0.0).astype(jnp.float32)
    base = (lane // block) * block
    for k in range(size // block):
        lo, hi = k * block, (k + 1) * block
        packed = [
            jnp.concatenate([work[t * groups + g, lo:hi, lo:hi] for g in range(groups)], axis=1)
            for t in range(tiles)
        ]
        inverse = [unit for _ in range(tiles)]
        scales = [jnp.ones((block, lanes), jnp.float32) for _ in range(tiles)]
        for j in range(block):
            for t in range(tiles):
                s, n = packed[t], inverse[t]
                column = jnp.take_along_axis(s, base + j, axis=1, mode="promise_in_bounds")
                pivot = column[j : j + 1, :]
                scales[t] = jnp.where(row == j, lax.rsqrt(pivot), scales[t])
                factor = jnp.where(row > j, column * (1.0 / pivot), 0.0)
                packed[t] = s - factor * s[j : j + 1, :]
                inverse[t] = n - factor * n[j : j + 1, :]
        packed = [jnp.where(lane % block >= row, s * c, 0.0) for s, c in zip(packed, scales)]
        inverse = [n * c for n, c in zip(inverse, scales)]
        for e in range(experts):
            t, g = e // groups, e % groups
            own = expert(e)
            work[e, lo:hi, lo:hi] = jnp.eye(block, dtype=jnp.float32)
            strip = exact_dot(
                inverse[t][:, g * block : (g + 1) * block], work[e, lo:hi, :], ((1,), (0,))
            )
            if lo:
                upper_ref[own, lo:hi, :lo] = jnp.zeros((block, lo), jnp.float32)
            upper_ref[own, lo:hi, lo:hi] = packed[t][:, g * block : (g + 1) * block]
            work[e, lo:hi, :] = strip
            if hi < size:
                upper_ref[own, lo:hi, hi:] = strip[:, hi:]
                work[e, hi:, lo:hi] = jnp.zeros((size - hi, block), jnp.float32)
                work[e, hi:, :] = work[e, hi:, :] - exact_dot(strip[:, hi:], strip, ((0,), (0,)))
    rows = lax.broadcasted_iota(jnp.int32, (size, size), 0)
    cols = lax.broadcasted_iota(jnp.int32, (size, size), 1)
    for e in range(experts):
        whole = jnp.where(rows >= cols, work[e], 0.0)
        high = whole.astype(jnp.bfloat16)
        high_ref[expert(e)] = high
        low_ref[expert(e)] = (whole - high.astype(jnp.float32)).astype(jnp.bfloat16)

    across = (((1,), (1,)), ((), ()))
    for away, rows_ref in zip((0, 1, -1, 2), row_refs):
        found = []
        for e in range(experts):
            a = rows_ref[e]
            found.append(
                lax.dot_general(a, high_ref[e], across, preferred_element_type=jnp.float32)
                + lax.dot_general(a, low_ref[e], across, preferred_element_type=jnp.float32)
            )
        for i, step in enumerate(NEAR):
            owner = lax.rem(y + step + SIDE, SIDE) * SIDE + lax.rem(x + away + SIDE, SIDE)
            own = slice(i * capacity, (i + 1) * capacity)
            codes_ref[owner] = jnp.concatenate([f[own] for f in found], axis=0).astype(
                codes_ref.dtype
            )


def factorize(at, mine, other, rows, capacity):
    count, _, half, _ = mine.shape
    experts, size = 2 * count, 2 * half
    square = (experts, size, size)
    return pl.pallas_call(
        functools.partial(factor_kernel, block=BLOCK, capacity=capacity),
        in_specs=[SCALARS] + [WHOLE] * (2 + len(rows)),
        out_specs=(WHOLE, WHOLE),
        out_shape=(
            jax.ShapeDtypeStruct(square, jnp.float32),
            jax.ShapeDtypeStruct((SIDE * SIDE, experts * capacity, size), jnp.bfloat16),
        ),
        scratch_shapes=[
            pltpu.VMEM(square, jnp.float32),
            pltpu.VMEM(square, jnp.bfloat16),
            pltpu.VMEM(square, jnp.bfloat16),
        ],
        compiler_params=params(),
        name="factorize",
    )(at, mine, other, *rows)


def slot_ranks(ids, first, experts):
    blocks, rows, _ = ids.shape
    wanted = first + jnp.arange(experts, dtype=jnp.int32)
    named = (jnp.swapaxes(ids, 1, 2)[:, :, None, :] == wanted[None, None, :, None]).any(axis=1)
    later = jnp.arange(rows)[:, None] < jnp.arange(rows)[None, :]
    rank = dot(named.reshape(-1, rows).astype(jnp.bfloat16), later.astype(jnp.bfloat16))
    return jnp.where(named, rank.reshape(named.shape), -1.0)


def sum_over_tok(mine, other):
    shape = mine.shape
    lanes = shape[-1]
    layers = lax.axis_size("z")
    mine = mine + shift(other, "c", 1)
    pieces = lax.all_to_all(mine.reshape(layers, -1, lanes), "z", 0, 0, tiled=True)
    mine = lax.all_gather(jnp.sum(pieces, axis=0), "z", tiled=True)
    other = shift(mine, "c", 1)
    return mine.reshape(shape), other.reshape(shape)


def local(tokens, first_factor, expert_ids):
    groups = lax.axis_size(("y", "x"))
    tok_ranks = lax.axis_size(("z", "c"))
    per_group, model_dim, rank_k = first_factor.shape
    tok_rows, top_k = expert_ids.shape
    experts = groups * per_group
    capacity = tok_rows * top_k * 5 // (4 * experts)
    gram_scale = experts / (top_k * tok_rows * tok_ranks * groups)
    y, x, core = lax.axis_index("y"), lax.axis_index("x"), lax.axis_index("c")
    at = jnp.stack([y, x, core]).astype(jnp.int32)

    depth = model_dim // 2
    thin = depth // tok_ranks
    thick = depth // 2
    middle = per_group // 2
    slices = lax.dynamic_slice_in_dim(first_factor, lax.axis_index(("z", "c")) * thin, thin, 1)
    slices_before, slices_after = shift(slices, "x", 1), shift(slices, "x", -1)
    slices_far = jnp.concatenate(
        [shift(slices_before[:middle], "x", 1), shift(slices_after[middle:], "x", -1)], axis=0
    )
    shared = lax.all_gather(jnp.stack([slices_before, slices_after, slices_far]), ("z", "c"))

    ids_before, ids_after = shift(expert_ids, "y", 1), shift(expert_ids, "y", -1)
    ids = jnp.stack([expert_ids, ids_before, ids_after, shift(ids_before, "y", 1)])
    tokens_before, tokens_after = shift(tokens, "y", 1), shift(tokens, "y", -1)
    thick_slice = lax.dynamic_slice_in_dim(first_factor, depth + core * thick, thick, 1)
    mine_before, mine_after = shift(thick_slice, "x", 1), shift(thick_slice, "x", -1)
    half_rows = tok_rows // 2
    tokens_far = [shift(tokens_before[:half_rows], "y", 1), shift(tokens_after[half_rows:], "y", -1)]
    mine_far = [shift(mine_before[:middle], "x", 1), shift(mine_after[middle:], "x", -1)]
    swap = lambda a: (a, shift(a, "c", 1))

    ranks = slot_ranks(ids, y * SIDE * per_group, SIDE * per_group)
    near = select(ranks[:2], tokens, [tokens_before], capacity)
    far = select(ranks[2:], tokens_after, tokens_far, capacity)

    def projected(step, factors, start, count, index=None):
        where = jnp.stack([(x + step) % SIDE, core]).astype(jnp.int32)
        return project(where, near, far, factors, per_group, start, count, index)

    rows_own = projected(0, [first_factor], 0, per_group)
    to_far = [
        projected(2, [shared, *swap(mine_far[i])], i * middle, middle, 2) for i in range(2)
    ]
    from_far = jnp.concatenate(
        [shift(shift(to_far[0], "x", 1), "x", 1), shift(shift(to_far[1], "x", -1), "x", -1)], axis=0
    )
    from_after = shift(projected(-1, [shared, *swap(mine_before)], 0, per_group, 0), "x", -1)
    from_before = shift(projected(1, [shared, *swap(mine_after)], 0, per_group, 1), "x", 1)
    rows = [rows_own, from_after, from_before, from_far]

    mine, other = sum_over_tok(*partial_grams(at, rows, gram_scale))
    upper, codes = factorize(at, mine, other, rows, capacity)
    returned = lax.all_to_all(codes, ("y", "x"), 0, 0, tiled=True)

    own_ranks = slot_ranks(expert_ids[None], 0, experts)[0]
    named = expert_ids.T[:, None, :] == jnp.arange(experts, dtype=jnp.int32)[None, :, None]
    slot = expert_ids.T * capacity + jnp.sum(jnp.where(named, own_ranks, 0.0), axis=1).astype(jnp.int32)
    gathered = returned.reshape(experts * capacity, rank_k)[slot.T.reshape(-1)]
    return (gathered.reshape(tok_rows, top_k, rank_k), upper)


def solution(mesh):
    fine = Mesh(mesh.devices.reshape(-1, 2, SIDE, SIDE), ("z", "c", "y", "x"))
    every = ("z", "c", "y", "x")
    in_specs = (P(every, None), P(("y", "x"), None, None), P(every, None))
    out_specs = (P(every, None, None), P(("y", "x"), None, None))
    return jax.shard_map(local, mesh=fine, in_specs=in_specs, out_specs=out_specs, check_vma=False)
```

```python
import functools

import jax
import jax.numpy as jnp
from jax import lax
from jax.experimental import pallas as pl
from jax.experimental.pallas import tpu as pltpu
from jax.sharding import Mesh
from jax.sharding import PartitionSpec as P

RIDGE = 0.1
BLOCK = 32
SIDE = 4
NEAR = (0, -1, 1, 2)
WHOLE = pl.BlockSpec(memory_space=pltpu.VMEM)
SCALARS = pl.BlockSpec(memory_space=pltpu.SMEM)


def params(mebibytes):
    return pltpu.CompilerParams(vmem_limit_bytes=mebibytes * 2**20)


def exact_dot(a, b, dims):
    return lax.dot_general(
        a, b, (dims, ((), ())), precision=lax.Precision.HIGHEST, preferred_element_type=jnp.float32
    )


def dot(a, b):
    return jnp.dot(a, b, preferred_element_type=jnp.float32)


def shift(array, axis, step):
    size = lax.axis_size(axis)
    return lax.ppermute(array, axis, [(i, (i + step) % size) for i in range(size)])


def select_kernel(rank_ref, first_ref, *rest, capacity):
    *second_refs, out_ref, picks = rest
    experts, tok_rows = rank_ref.shape[1:]

    @pl.when(pl.program_id(0) == 0)
    def _():
        slots = lax.broadcasted_iota(jnp.int32, (capacity, tok_rows), 0).astype(jnp.float32)
        for source in range(2):
            for pair in range(experts // 2):
                both = [
                    jnp.where(rank_ref[source, e : e + 1, :] == slots, 1.0, 0.0)
                    for e in (2 * pair, 2 * pair + 1)
                ]
                picks[source, pair * 2 * capacity : (pair + 1) * 2 * capacity, :] = jnp.concatenate(
                    both, axis=0
                ).astype(jnp.bfloat16)

    blocks = (first_ref[...], jnp.concatenate([r[...] for r in second_refs], axis=0))
    step = 8
    for e in range(0, experts, step):
        rows = slice(e * capacity, (e + step) * capacity)
        found = [dot(picks[source, rows, :], blocks[source]) for source in range(2)]
        for i in range(step):
            own = slice(i * capacity, (i + 1) * capacity)
            out_ref[e + i] = jnp.concatenate([found[0][own], found[1][own]], axis=0).astype(
                out_ref.dtype
            )


def select(ranks, first, second, capacity, columns=512):
    _, experts, tok_rows = ranks.shape
    width = first.shape[1]
    columns = min(columns, width)
    return pl.pallas_call(
        functools.partial(select_kernel, capacity=capacity),
        grid=(width // columns,),
        in_specs=[pl.BlockSpec(ranks.shape, lambda i: (0, 0, 0))]
        + [pl.BlockSpec((a.shape[0], columns), lambda i: (0, i)) for a in (first, *second)],
        out_specs=pl.BlockSpec((experts, 2 * capacity, columns), lambda i: (0, 0, i)),
        out_shape=jax.ShapeDtypeStruct((experts, 2 * capacity, width), first.dtype),
        scratch_shapes=[pltpu.VMEM((2, experts * capacity, tok_rows), jnp.bfloat16)],
        compiler_params=params(24),
        cost_estimate=pl.CostEstimate(
            flops=4 * experts * capacity * tok_rows * width, bytes_accessed=2**24, transcendentals=0
        ),
        name="select",
    )(ranks, first, *second)


def project_own_kernel(at_ref, near_ref, far_ref, factor_ref, out_ref):
    rows = jnp.concatenate([near_ref[0], far_ref[0]], axis=0)
    out_ref[0] = dot(rows, factor_ref[0]).astype(out_ref.dtype)


def project_kernel(at_ref, near_ref, far_ref, shared_ref, mine_ref, other_ref, out_ref):
    rows = jnp.concatenate([near_ref[0], far_ref[0]], axis=0)
    shared = shared_ref[...]
    shared = shared.reshape(-1, shared.shape[-1])
    depth = shared.shape[0]
    half = mine_ref.shape[1]
    low, high = rows[:, depth : depth + half], rows[:, depth + half :]
    first = at_ref[1] == 0
    total = dot(rows[:, :depth], shared)
    total += dot(jnp.where(first, low, high), mine_ref[0])
    total += dot(jnp.where(first, high, low), other_ref[0])
    out_ref[0] = total.astype(out_ref.dtype)


def project(at, near, far, factors, per_group, start, count, index=None):
    width = near.shape[2]
    rank_k = factors[0].shape[-1]
    row_spec = lambda rows: pl.BlockSpec(
        (1, rows, width), lambda i, at: (at[0] * per_group + start + i, 0, 0)
    )
    plain = lambda a: pl.BlockSpec((1,) + a.shape[1:], lambda i, at: (i, 0, 0))
    if index is None:
        kernel, specs = project_own_kernel, [plain(factors[0])]
    else:
        shared = factors[0]
        kernel = project_kernel
        specs = [
            pl.BlockSpec(
                (shared.shape[0], 1, 1) + shared.shape[3:],
                lambda i, at: (0, index, start + i, 0, 0),
            ),
            plain(factors[1]),
            plain(factors[2]),
        ]
    rows = near.shape[1] + far.shape[1]
    return pl.pallas_call(
        kernel,
        grid_spec=pltpu.PrefetchScalarGridSpec(
            num_scalar_prefetch=1,
            grid=(count,),
            in_specs=[row_spec(near.shape[1]), row_spec(far.shape[1])] + specs,
            out_specs=pl.BlockSpec((1, rows, rank_k), lambda i, at: (i, 0, 0)),
        ),
        out_shape=jax.ShapeDtypeStruct((count, rows, rank_k), near.dtype),
        compiler_params=params(24),
        cost_estimate=pl.CostEstimate(
            flops=2 * count * rows * width * rank_k,
            bytes_accessed=2 * count * width * (rows + rank_k),
            transcendentals=0,
        ),
        name="project",
    )(at, near, far, *factors)


def gram_kernel(at_ref, *refs, scale):
    *row_refs, mine_ref, other_ref = refs
    count, _, half, _ = mine_ref.shape
    core = at_ref[2]
    for out_ref, turn in ((mine_ref, core), (other_ref, 1 - core)):
        for i in range(count):
            rows = jnp.concatenate([r[turn * count + i] for r in row_refs], axis=0)
            lower, upper = rows[:, :half], rows[:, half:]
            transposed = ((0,), (0,))
            pairs = ((lower, lower), (lower, upper), (upper, upper))
            for block, (a, b) in enumerate(pairs):
                out_ref[i, block] = scale * lax.dot_general(
                    a, b, (transposed, ((), ())), preferred_element_type=jnp.float32
                )


def partial_grams(at, rows, scale):
    experts, _, rank_k = rows[0].shape
    half = jax.ShapeDtypeStruct((experts // 2, 3, rank_k // 2, rank_k // 2), jnp.float32)
    return pl.pallas_call(
        functools.partial(gram_kernel, scale=scale),
        in_specs=[SCALARS] + [WHOLE] * len(rows),
        out_specs=(WHOLE, WHOLE),
        out_shape=(half, half),
        compiler_params=params(16),
        name="grams",
    )(at, *rows)


def factor_kernel(at_ref, mine_ref, other_ref, *refs, block, capacity):
    *row_refs, upper_ref, codes_ref, work, high_ref, low_ref = refs
    count, _, half, _ = mine_ref.shape
    experts = 2 * count
    size = 2 * half
    lanes = 128
    groups = lanes // block
    tiles = experts // groups
    y, x, core = at_ref[0], at_ref[1], at_ref[2]
    expert = lambda e: core * count + e if e < count else (1 - core) * count + e - count
    rows_h = lax.broadcasted_iota(jnp.int32, (half, half), 0)
    cols_h = lax.broadcasted_iota(jnp.int32, (half, half), 1)
    ridge_h = jnp.where(rows_h == cols_h, RIDGE, 0.0).astype(jnp.float32)
    for e in range(experts):
        source, i = (mine_ref, e) if e < count else (other_ref, e - count)
        work[e, :half, :half] = source[i, 0] + ridge_h
        work[e, :half, half:] = source[i, 1]
        work[e, half:, half:] = source[i, 2] + ridge_h
    lane = lax.broadcasted_iota(jnp.int32, (block, lanes), 1)
    row = lax.broadcasted_iota(jnp.int32, (block, lanes), 0)
    unit = jnp.where(lane % block == row, 1.0, 0.0).astype(jnp.float32)
    base = (lane // block) * block
    for k in range(size // block):
        lo, hi = k * block, (k + 1) * block
        packed = [
            jnp.concatenate([work[t * groups + g, lo:hi, lo:hi] for g in range(groups)], axis=1)
            for t in range(tiles)
        ]
        inverse = [unit for _ in range(tiles)]
        scales = [jnp.ones((block, lanes), jnp.float32) for _ in range(tiles)]
        for j in range(block):
            for t in range(tiles):
                s, n = packed[t], inverse[t]
                column = jnp.take_along_axis(s, base + j, axis=1, mode="promise_in_bounds")
                pivot = column[j : j + 1, :]
                scales[t] = jnp.where(row == j, lax.rsqrt(pivot), scales[t])
                factor = jnp.where(row > j, column * (1.0 / pivot), 0.0)
                packed[t] = s - factor * s[j : j + 1, :]
                inverse[t] = n - factor * n[j : j + 1, :]
        packed = [jnp.where(lane % block >= row, s * c, 0.0) for s, c in zip(packed, scales)]
        inverse = [n * c for n, c in zip(inverse, scales)]
        for e in range(experts):
            t, g = e // groups, e % groups
            own = expert(e)
            work[e, lo:hi, lo:hi] = jnp.eye(block, dtype=jnp.float32)
            strip = exact_dot(
                inverse[t][:, g * block : (g + 1) * block], work[e, lo:hi, :], ((1,), (0,))
            )
            if lo:
                upper_ref[own, lo:hi, :lo] = jnp.zeros((block, lo), jnp.float32)
            upper_ref[own, lo:hi, lo:hi] = packed[t][:, g * block : (g + 1) * block]
            work[e, lo:hi, :] = strip
            if hi < size:
                upper_ref[own, lo:hi, hi:] = strip[:, hi:]
                work[e, hi:, lo:hi] = jnp.zeros((size - hi, block), jnp.float32)
                work[e, hi:, :] = work[e, hi:, :] - exact_dot(strip[:, hi:], strip, ((0,), (0,)))
    rows = lax.broadcasted_iota(jnp.int32, (size, size), 0)
    cols = lax.broadcasted_iota(jnp.int32, (size, size), 1)
    for e in range(experts):
        whole = jnp.where(rows >= cols, work[e], 0.0)
        high = whole.astype(jnp.bfloat16)
        high_ref[expert(e)] = high
        low_ref[expert(e)] = (whole - high.astype(jnp.float32)).astype(jnp.bfloat16)

    across = (((1,), (1,)), ((), ()))
    for away, rows_ref in zip((0, 1, -1, 2), row_refs):
        found = []
        for e in range(experts):
            a = rows_ref[e]
            found.append(
                lax.dot_general(a, high_ref[e], across, preferred_element_type=jnp.float32)
                + lax.dot_general(a, low_ref[e], across, preferred_element_type=jnp.float32)
            )
        for i, step in enumerate(NEAR):
            owner = lax.rem(y + step + SIDE, SIDE) * SIDE + lax.rem(x + away + SIDE, SIDE)
            own = slice(i * capacity, (i + 1) * capacity)
            codes_ref[owner] = jnp.concatenate([f[own] for f in found], axis=0).astype(
                codes_ref.dtype
            )


def factorize(at, mine, other, rows, capacity):
    count, _, half, _ = mine.shape
    experts, size = 2 * count, 2 * half
    square = (experts, size, size)
    return pl.pallas_call(
        functools.partial(factor_kernel, block=BLOCK, capacity=capacity),
        in_specs=[SCALARS] + [WHOLE] * (2 + len(rows)),
        out_specs=(WHOLE, WHOLE),
        out_shape=(
            jax.ShapeDtypeStruct(square, jnp.float32),
            jax.ShapeDtypeStruct((SIDE * SIDE, experts * capacity, size), jnp.bfloat16),
        ),
        scratch_shapes=[
            pltpu.VMEM(square, jnp.float32),
            pltpu.VMEM(square, jnp.bfloat16),
            pltpu.VMEM(square, jnp.bfloat16),
        ],
        compiler_params=params(24),
        name="factorize",
    )(at, mine, other, *rows)


def slot_ranks(ids, first, experts):
    blocks, rows, _ = ids.shape
    wanted = first + jnp.arange(experts, dtype=jnp.int32)
    named = (jnp.swapaxes(ids, 1, 2)[:, :, None, :] == wanted[None, None, :, None]).any(axis=1)
    later = jnp.arange(rows)[:, None] < jnp.arange(rows)[None, :]
    rank = dot(named.reshape(-1, rows).astype(jnp.bfloat16), later.astype(jnp.bfloat16))
    return jnp.where(named, rank.reshape(named.shape), -1.0)


def sum_over_tok(mine, other):
    shape = mine.shape
    lanes = shape[-1]
    layers = lax.axis_size("z")
    mine = mine + shift(other, "c", 1)
    pieces = lax.all_to_all(mine.reshape(layers, -1, lanes), "z", 0, 0, tiled=True)
    mine = lax.all_gather(jnp.sum(pieces, axis=0), "z", tiled=True)
    other = shift(mine, "c", 1)
    return mine.reshape(shape), other.reshape(shape)


def local(tokens, first_factor, expert_ids):
    groups = lax.axis_size(("y", "x"))
    tok_ranks = lax.axis_size(("z", "c"))
    per_group, model_dim, rank_k = first_factor.shape
    tok_rows, top_k = expert_ids.shape
    experts = groups * per_group
    capacity = tok_rows * top_k * 5 // (4 * experts)
    gram_scale = experts / (top_k * tok_rows * tok_ranks * groups)
    y, x, core = lax.axis_index("y"), lax.axis_index("x"), lax.axis_index("c")
    at = jnp.stack([y, x, core]).astype(jnp.int32)

    depth = model_dim // 2
    thin = depth // tok_ranks
    thick = depth // 2
    middle = per_group // 2
    half_rows = tok_rows // 2
    tied = lax.optimization_barrier
    slices = lax.dynamic_slice_in_dim(first_factor, lax.axis_index(("z", "c")) * thin, thin, 1)
    slices_before, slices_after, ids_before, ids_after = tied(
        (
            shift(slices, "x", 1),
            shift(slices, "x", -1),
            shift(expert_ids, "y", 1),
            shift(expert_ids, "y", -1),
        )
    )
    slices_low, slices_high = shift(slices_before[:middle], "x", 1), shift(slices_after[middle:], "x", -1)
    ids_far = shift(ids_before, "y", 1)
    thick_slice = lax.dynamic_slice_in_dim(first_factor, depth + core * thick, thick, 1)
    thick_slice, tokens_out, slices_low, slices_high, ids_far = tied(
        (thick_slice, tokens, slices_low, slices_high, ids_far)
    )
    slices_far = jnp.concatenate([slices_low, slices_high], axis=0)
    shared = lax.all_gather(jnp.stack([slices_before, slices_after, slices_far]), ("z", "c"))
    tokens_before, tokens_after, mine_before, mine_after = tied(
        (
            shift(tokens_out, "y", 1),
            shift(tokens_out, "y", -1),
            shift(thick_slice, "x", 1),
            shift(thick_slice, "x", -1),
        )
    )
    tokens_far = [shift(tokens_before[:half_rows], "y", 1), shift(tokens_after[half_rows:], "y", -1)]
    mine_far = [shift(mine_before[:middle], "x", 1), shift(mine_after[middle:], "x", -1)]
    ids = jnp.stack([expert_ids, ids_before, ids_after, ids_far])
    ranks = slot_ranks(ids, y * SIDE * per_group, SIDE * per_group)
    near = select(ranks[:2], tokens, [tokens_before], capacity)
    near, mine_before, mine_after, *far = tied(
        (near, mine_before, mine_after, *tokens_far, *mine_far)
    )
    tokens_far, mine_far = far[:2], far[2:]
    swap = lambda a: (a, shift(a, "c", 1))

    far = select(ranks[2:], tokens_after, tokens_far, capacity)

    def projected(step, factors, start, count, index=None):
        where = jnp.stack([(x + step) % SIDE, core]).astype(jnp.int32)
        return project(where, near, far, factors, per_group, start, count, index)

    rows_own = projected(0, [first_factor], 0, per_group)
    to_far = [
        projected(2, [shared, *swap(mine_far[i])], i * middle, middle, 2) for i in range(2)
    ]
    from_far = jnp.concatenate(
        [shift(shift(to_far[0], "x", 1), "x", 1), shift(shift(to_far[1], "x", -1), "x", -1)], axis=0
    )
    from_after = shift(projected(-1, [shared, *swap(mine_before)], 0, per_group, 0), "x", -1)
    from_before = shift(projected(1, [shared, *swap(mine_after)], 0, per_group, 1), "x", 1)
    rows = [rows_own, from_after, from_before, from_far]

    mine, other = sum_over_tok(*partial_grams(at, rows, gram_scale))
    upper, codes = factorize(at, mine, other, rows, capacity)
    returned = lax.all_to_all(codes, ("y", "x"), 0, 0, tiled=True)

    own_ranks = slot_ranks(expert_ids[None], 0, experts)[0]
    named = expert_ids.T[:, None, :] == jnp.arange(experts, dtype=jnp.int32)[None, :, None]
    slot = expert_ids.T * capacity + jnp.sum(jnp.where(named, own_ranks, 0.0), axis=1).astype(jnp.int32)
    gathered = returned.reshape(experts * capacity, rank_k)[slot.T.reshape(-1)]
    return (gathered.reshape(tok_rows, top_k, rank_k), upper)


def solution(mesh):
    fine = Mesh(mesh.devices.reshape(-1, 2, SIDE, SIDE), ("z", "c", "y", "x"))
    every = ("z", "c", "y", "x")
    in_specs = (P(every, None), P(("y", "x"), None, None), P(every, None))
    out_specs = (P(every, None, None), P(("y", "x"), None, None))
    return jax.shard_map(local, mesh=fine, in_specs=in_specs, out_specs=out_specs, check_vma=False)
```

```python
import functools

import jax
import jax.numpy as jnp
from jax import lax
from jax.experimental import pallas as pl
from jax.experimental.pallas import tpu as pltpu
from jax.sharding import Mesh
from jax.sharding import PartitionSpec as P

RIDGE = 0.1
BLOCK = 32
SIDE = 4
NEAR = (0, -1, 1, 2)
WHOLE = pl.BlockSpec(memory_space=pltpu.VMEM)
SCALARS = pl.BlockSpec(memory_space=pltpu.SMEM)


def params(mebibytes):
    return pltpu.CompilerParams(vmem_limit_bytes=mebibytes * 2**20)


def exact_dot(a, b, dims):
    return lax.dot_general(
        a, b, (dims, ((), ())), precision=lax.Precision.HIGHEST, preferred_element_type=jnp.float32
    )


def dot(a, b):
    return jnp.dot(a, b, preferred_element_type=jnp.float32)


def shift(array, axis, step):
    size = lax.axis_size(axis)
    return lax.ppermute(array, axis, [(i, (i + step) % size) for i in range(size)])


def select_kernel(rank_ref, first_ref, *rest, capacity):
    *second_refs, out_ref, picks = rest
    experts, tok_rows = rank_ref.shape[1:]

    @pl.when(pl.program_id(0) == 0)
    def _():
        slots = lax.broadcasted_iota(jnp.int32, (capacity, tok_rows), 0).astype(jnp.float32)
        for source in range(2):
            for pair in range(experts // 2):
                both = [
                    jnp.where(rank_ref[source, e : e + 1, :] == slots, 1.0, 0.0)
                    for e in (2 * pair, 2 * pair + 1)
                ]
                picks[source, pair * 2 * capacity : (pair + 1) * 2 * capacity, :] = jnp.concatenate(
                    both, axis=0
                ).astype(jnp.bfloat16)

    blocks = (first_ref[...], jnp.concatenate([r[...] for r in second_refs], axis=0))
    step = 8
    for e in range(0, experts, step):
        rows = slice(e * capacity, (e + step) * capacity)
        found = [dot(picks[source, rows, :], blocks[source]) for source in range(2)]
        for i in range(step):
            own = slice(i * capacity, (i + 1) * capacity)
            out_ref[e + i] = jnp.concatenate([found[0][own], found[1][own]], axis=0).astype(
                out_ref.dtype
            )


def select(ranks, first, second, capacity, width, columns=512):
    _, experts, tok_rows = ranks.shape
    columns = min(columns, width)
    return pl.pallas_call(
        functools.partial(select_kernel, capacity=capacity),
        grid=(width // columns,),
        in_specs=[pl.BlockSpec(ranks.shape, lambda i: (0, 0, 0))]
        + [pl.BlockSpec((a.shape[0], columns), lambda i: (0, i)) for a in (first, *second)],
        out_specs=pl.BlockSpec((experts, 2 * capacity, columns), lambda i: (0, 0, i)),
        out_shape=jax.ShapeDtypeStruct((experts, 2 * capacity, width), first.dtype),
        scratch_shapes=[pltpu.VMEM((2, experts * capacity, tok_rows), jnp.bfloat16)],
        compiler_params=params(56),
        cost_estimate=pl.CostEstimate(
            flops=4 * experts * capacity * tok_rows * width, bytes_accessed=2**24, transcendentals=0
        ),
        name="select",
    )(ranks, first, *second)


def project_own_kernel(at_ref, near_ref, far_ref, factor_ref, out_ref):
    for i in range(out_ref.shape[0]):
        rows = jnp.concatenate([near_ref[i], far_ref[i]], axis=0)
        out_ref[i] = dot(rows, factor_ref[i]).astype(out_ref.dtype)


def project_kernel(at_ref, near_ref, far_ref, shared_ref, mine_ref, other_ref, out_ref):
    slices, _, _, thin, rank_k = shared_ref.shape
    half = mine_ref.shape[1]
    depth = slices * thin
    first = at_ref[1] == 0
    for i in range(out_ref.shape[0]):
        rows = jnp.concatenate([near_ref[i], far_ref[i]], axis=0)
        low, high = rows[:, depth : depth + half], rows[:, depth + half :]
        total = dot(rows[:, :depth], shared_ref[:, 0, i].reshape(depth, rank_k))
        total += dot(jnp.where(first, low, high), mine_ref[i])
        total += dot(jnp.where(first, high, low), other_ref[i])
        out_ref[i] = total.astype(out_ref.dtype)


def project(at, near, far, factors, per_group, start, count, index=None, step=2):
    width = near.shape[2]
    rank_k = factors[0].shape[-1]
    row_spec = lambda rows: pl.BlockSpec(
        (step, rows, width), lambda i, at: ((at[0] * per_group + start) // step + i, 0, 0)
    )
    plain = lambda a: pl.BlockSpec((step,) + a.shape[1:], lambda i, at: (i, 0, 0))
    if index is None:
        kernel, specs = project_own_kernel, [plain(factors[0])]
    else:
        shared = factors[0]
        kernel = project_kernel
        specs = [
            pl.BlockSpec(
                (shared.shape[0], 1, step) + shared.shape[3:],
                lambda i, at: (0, index, start // step + i, 0, 0),
            ),
            plain(factors[1]),
            plain(factors[2]),
        ]
    rows = near.shape[1] + far.shape[1]
    return pl.pallas_call(
        kernel,
        grid_spec=pltpu.PrefetchScalarGridSpec(
            num_scalar_prefetch=1,
            grid=(count // step,),
            in_specs=[row_spec(near.shape[1]), row_spec(far.shape[1])] + specs,
            out_specs=pl.BlockSpec((step, rows, rank_k), lambda i, at: (i, 0, 0)),
        ),
        out_shape=jax.ShapeDtypeStruct((count, rows, rank_k), near.dtype),
        compiler_params=params(56),
        cost_estimate=pl.CostEstimate(
            flops=2 * count * rows * width * rank_k,
            bytes_accessed=2 * count * width * (rows + rank_k),
            transcendentals=0,
        ),
        name="project",
    )(at, near, far, *factors)


def gram_kernel(at_ref, *refs, scale):
    *row_refs, mine_ref, other_ref = refs
    count, _, half, _ = mine_ref.shape
    core = at_ref[2]
    for out_ref, turn in ((mine_ref, core), (other_ref, 1 - core)):
        for i in range(count):
            rows = jnp.concatenate([r[turn * count + i] for r in row_refs], axis=0)
            lower, upper = rows[:, :half], rows[:, half:]
            transposed = ((0,), (0,))
            pairs = ((lower, lower), (lower, upper), (upper, upper))
            for block, (a, b) in enumerate(pairs):
                out_ref[i, block] = scale * lax.dot_general(
                    a, b, (transposed, ((), ())), preferred_element_type=jnp.float32
                )


def partial_grams(at, rows, scale):
    experts, _, rank_k = rows[0].shape
    half = jax.ShapeDtypeStruct((experts // 2, 3, rank_k // 2, rank_k // 2), jnp.float32)
    return pl.pallas_call(
        functools.partial(gram_kernel, scale=scale),
        in_specs=[SCALARS] + [WHOLE] * len(rows),
        out_specs=(WHOLE, WHOLE),
        out_shape=(half, half),
        compiler_params=params(16),
        name="grams",
    )(at, *rows)


def factor_kernel(at_ref, mine_ref, other_ref, *refs, block, capacity):
    *row_refs, upper_ref, codes_ref, work, high_ref, low_ref = refs
    count, _, half, _ = mine_ref.shape
    experts = 2 * count
    size = 2 * half
    lanes = 128
    groups = lanes // block
    tiles = experts // groups
    y, x, core = at_ref[0], at_ref[1], at_ref[2]
    expert = lambda e: core * count + e if e < count else (1 - core) * count + e - count
    rows_h = lax.broadcasted_iota(jnp.int32, (half, half), 0)
    cols_h = lax.broadcasted_iota(jnp.int32, (half, half), 1)
    ridge_h = jnp.where(rows_h == cols_h, RIDGE, 0.0).astype(jnp.float32)
    for e in range(experts):
        source, i = (mine_ref, e) if e < count else (other_ref, e - count)
        work[e, :half, :half] = source[i, 0] + ridge_h
        work[e, :half, half:] = source[i, 1]
        work[e, half:, half:] = source[i, 2] + ridge_h
    lane = lax.broadcasted_iota(jnp.int32, (block, lanes), 1)
    row = lax.broadcasted_iota(jnp.int32, (block, lanes), 0)
    unit = jnp.where(lane % block == row, 1.0, 0.0).astype(jnp.float32)
    base = (lane // block) * block
    for k in range(size // block):
        lo, hi = k * block, (k + 1) * block
        packed = [
            jnp.concatenate([work[t * groups + g, lo:hi, lo:hi] for g in range(groups)], axis=1)
            for t in range(tiles)
        ]
        inverse = [unit for _ in range(tiles)]
        scales = [jnp.ones((block, lanes), jnp.float32) for _ in range(tiles)]
        for j in range(block):
            for t in range(tiles):
                s, n = packed[t], inverse[t]
                column = jnp.take_along_axis(s, base + j, axis=1, mode="promise_in_bounds")
                pivot = column[j : j + 1, :]
                scales[t] = jnp.where(row == j, lax.rsqrt(pivot), scales[t])
                factor = jnp.where(row > j, column * (1.0 / pivot), 0.0)
                packed[t] = s - factor * s[j : j + 1, :]
                inverse[t] = n - factor * n[j : j + 1, :]
        packed = [jnp.where(lane % block >= row, s * c, 0.0) for s, c in zip(packed, scales)]
        inverse = [n * c for n, c in zip(inverse, scales)]
        for e in range(experts):
            t, g = e // groups, e % groups
            own = expert(e)
            work[e, lo:hi, lo:hi] = jnp.eye(block, dtype=jnp.float32)
            strip = exact_dot(
                inverse[t][:, g * block : (g + 1) * block], work[e, lo:hi, :], ((1,), (0,))
            )
            if lo:
                upper_ref[own, lo:hi, :lo] = jnp.zeros((block, lo), jnp.float32)
            upper_ref[own, lo:hi, lo:hi] = packed[t][:, g * block : (g + 1) * block]
            work[e, lo:hi, :] = strip
            if hi < size:
                upper_ref[own, lo:hi, hi:] = strip[:, hi:]
                work[e, hi:, lo:hi] = jnp.zeros((size - hi, block), jnp.float32)
                work[e, hi:, :] = work[e, hi:, :] - exact_dot(strip[:, hi:], strip, ((0,), (0,)))
    rows = lax.broadcasted_iota(jnp.int32, (size, size), 0)
    cols = lax.broadcasted_iota(jnp.int32, (size, size), 1)
    for e in range(experts):
        whole = jnp.where(rows >= cols, work[e], 0.0)
        high = whole.astype(jnp.bfloat16)
        high_ref[expert(e)] = high
        low_ref[expert(e)] = (whole - high.astype(jnp.float32)).astype(jnp.bfloat16)

    across = (((1,), (1,)), ((), ()))
    for away, rows_ref in zip((0, 1, -1, 2), row_refs):
        found = []
        for e in range(experts):
            a = rows_ref[e]
            found.append(
                lax.dot_general(a, high_ref[e], across, preferred_element_type=jnp.float32)
                + lax.dot_general(a, low_ref[e], across, preferred_element_type=jnp.float32)
            )
        for i, step in enumerate(NEAR):
            owner = lax.rem(y + step + SIDE, SIDE) * SIDE + lax.rem(x + away + SIDE, SIDE)
            own = slice(i * capacity, (i + 1) * capacity)
            codes_ref[owner] = jnp.concatenate([f[own] for f in found], axis=0).astype(
                codes_ref.dtype
            )


def factorize(at, mine, other, rows, capacity):
    count, _, half, _ = mine.shape
    experts, size = 2 * count, 2 * half
    square = (experts, size, size)
    return pl.pallas_call(
        functools.partial(factor_kernel, block=BLOCK, capacity=capacity),
        in_specs=[SCALARS] + [WHOLE] * (2 + len(rows)),
        out_specs=(WHOLE, WHOLE),
        out_shape=(
            jax.ShapeDtypeStruct(square, jnp.float32),
            jax.ShapeDtypeStruct((SIDE * SIDE, experts * capacity, size), jnp.bfloat16),
        ),
        scratch_shapes=[
            pltpu.VMEM(square, jnp.float32),
            pltpu.VMEM(square, jnp.bfloat16),
            pltpu.VMEM(square, jnp.bfloat16),
        ],
        compiler_params=params(24),
        name="factorize",
    )(at, mine, other, *rows)


def slot_ranks(ids, first, experts):
    blocks, rows, _ = ids.shape
    wanted = first + jnp.arange(experts, dtype=jnp.int32)
    named = (jnp.swapaxes(ids, 1, 2)[:, :, None, :] == wanted[None, None, :, None]).any(axis=1)
    later = jnp.arange(rows)[:, None] < jnp.arange(rows)[None, :]
    rank = dot(named.reshape(-1, rows).astype(jnp.bfloat16), later.astype(jnp.bfloat16))
    return jnp.where(named, rank.reshape(named.shape), -1.0)


def sum_over_tok(mine, other):
    shape = mine.shape
    lanes = shape[-1]
    layers = lax.axis_size("z")
    mine = mine + shift(other, "c", 1)
    pieces = lax.all_to_all(mine.reshape(layers, -1, lanes), "z", 0, 0, tiled=True)
    mine = lax.all_gather(jnp.sum(pieces, axis=0), "z", tiled=True)
    other = shift(mine, "c", 1)
    return mine.reshape(shape), other.reshape(shape)


def local(tokens, first_factor, expert_ids):
    groups = lax.axis_size(("y", "x"))
    tok_ranks = lax.axis_size(("z", "c"))
    per_group, model_dim, rank_k = first_factor.shape
    tok_rows, top_k = expert_ids.shape
    experts = groups * per_group
    capacity = tok_rows * top_k * 5 // (4 * experts)
    gram_scale = experts / (top_k * tok_rows * tok_ranks * groups)
    y, x, core = lax.axis_index("y"), lax.axis_index("x"), lax.axis_index("c")
    at = jnp.stack([y, x, core]).astype(jnp.int32)

    depth = model_dim // 2
    thin = depth // tok_ranks
    thick = depth // 2
    middle = per_group // 2
    half_rows = tok_rows // 2
    tied = lax.optimization_barrier
    lanes = 128
    tagged = jnp.concatenate(
        [tokens, jnp.pad(expert_ids.astype(tokens.dtype), ((0, 0), (0, lanes - top_k)))], axis=1
    )
    slices = lax.dynamic_slice_in_dim(first_factor, lax.axis_index(("z", "c")) * thin, thin, 1)
    thick_slice = lax.dynamic_slice_in_dim(first_factor, depth + core * thick, thick, 1)
    slices_before, slices_after, slices_far = shift(slices, "x", 1), shift(slices, "x", -1), shift(slices, "x", 2)
    tagged, thick_slice, slices_before, slices_after, slices_far = tied(
        (tagged, thick_slice, slices_before, slices_after, slices_far)
    )
    shared = lax.all_gather(jnp.stack([slices_before, slices_after, slices_far]), ("z", "c"))
    tokens_before, tokens_after, mine_before, mine_after = tied(
        (
            shift(tagged, "y", 1),
            shift(tagged, "y", -1),
            shift(thick_slice, "x", 1),
            shift(thick_slice, "x", -1),
        )
    )
    tokens_far = [shift(tokens_before[:half_rows], "y", 1), shift(tokens_after[half_rows:], "y", -1)]
    mine_far = [shift(mine_before[:middle], "x", 1), shift(mine_after[middle:], "x", -1)]
    ids_of = lambda a: a[:, model_dim : model_dim + top_k].astype(jnp.int32)
    first_of = y * SIDE * per_group
    near_ids = jnp.stack([expert_ids, ids_of(tokens_before)])
    near = select(
        slot_ranks(near_ids, first_of, SIDE * per_group),
        tokens,
        [tokens_before],
        capacity,
        model_dim,
    )
    near, mine_before, mine_after, *arrived = tied(
        (near, mine_before, mine_after, *tokens_far, *mine_far)
    )
    tokens_far, mine_far = arrived[:2], arrived[2:]
    far_ids = jnp.stack(
        [ids_of(tokens_after), jnp.concatenate([ids_of(a) for a in tokens_far], axis=0)]
    )
    far = select(
        slot_ranks(far_ids, first_of, SIDE * per_group),
        tokens_after,
        tokens_far,
        capacity,
        model_dim,
    )
    swap = lambda a: (a, shift(a, "c", 1))

    def projected(step, factors, start, count, index=None):
        where = jnp.stack([(x + step) % SIDE, core]).astype(jnp.int32)
        return project(where, near, far, factors, per_group, start, count, index)

    to_far = [
        projected(2, [shared, *swap(mine_far[i])], i * middle, middle, 2) for i in range(2)
    ]
    from_after = shift(projected(-1, [shared, *swap(mine_before)], 0, per_group, 0), "x", -1)
    relay = [shift(to_far[0], "x", 1), shift(to_far[1], "x", -1)]
    near, far, *relay = tied((near, far, *relay))
    from_far = [shift(relay[0], "x", 1), shift(relay[1], "x", -1)]
    from_before = shift(projected(1, [shared, *swap(mine_after)], 0, per_group, 1), "x", 1)
    rows_own = projected(0, [first_factor], 0, per_group)
    from_far = jnp.concatenate(from_far, axis=0)
    rows_own, expert_ids = tied((rows_own, expert_ids))
    rows = [rows_own, from_after, from_before, from_far]

    mine, other = sum_over_tok(*partial_grams(at, rows, gram_scale))
    upper, codes = factorize(at, mine, other, rows, capacity)
    returned = lax.all_to_all(codes, ("y", "x"), 0, 0, tiled=True)

    own_ranks = slot_ranks(expert_ids[None], 0, experts)[0]
    named = expert_ids.T[:, None, :] == jnp.arange(experts, dtype=jnp.int32)[None, :, None]
    slot = expert_ids.T * capacity + jnp.sum(jnp.where(named, own_ranks, 0.0), axis=1).astype(jnp.int32)
    gathered = returned.reshape(experts * capacity, rank_k)[slot.T.reshape(-1)]
    return (gathered.reshape(tok_rows, top_k, rank_k), upper)


def solution(mesh):
    fine = Mesh(mesh.devices.reshape(-1, 2, SIDE, SIDE), ("z", "c", "y", "x"))
    every = ("z", "c", "y", "x")
    in_specs = (P(every, None), P(("y", "x"), None, None), P(every, None))
    out_specs = (P(every, None, None), P(("y", "x"), None, None))
    return jax.shard_map(local, mesh=fine, in_specs=in_specs, out_specs=out_specs, check_vma=False)
```

```python
import functools

import jax
import jax.numpy as jnp
from jax import lax
from jax.experimental import pallas as pl
from jax.experimental.pallas import tpu as pltpu
from jax.sharding import Mesh
from jax.sharding import PartitionSpec as P

RIDGE = 0.1
BLOCK = 32
SIDE = 4
NEAR = (0, -1, 1, 2)
WHOLE = pl.BlockSpec(memory_space=pltpu.VMEM)
SCALARS = pl.BlockSpec(memory_space=pltpu.SMEM)


def params(mebibytes):
    return pltpu.CompilerParams(vmem_limit_bytes=mebibytes * 2**20)


def exact_dot(a, b, dims):
    return lax.dot_general(
        a, b, (dims, ((), ())), precision=lax.Precision.HIGHEST, preferred_element_type=jnp.float32
    )


def dot(a, b):
    return jnp.dot(a, b, preferred_element_type=jnp.float32)


def shift(array, axis, step):
    size = lax.axis_size(axis)
    return lax.ppermute(array, axis, [(i, (i + step) % size) for i in range(size)])


def select_kernel(rank_ref, first_ref, *rest, capacity):
    *second_refs, out_ref, picks = rest
    experts, tok_rows = rank_ref.shape[1:]

    @pl.when(pl.program_id(0) == 0)
    def _():
        slots = lax.broadcasted_iota(jnp.int32, (capacity, tok_rows), 0).astype(jnp.float32)
        for source in range(2):
            for pair in range(experts // 2):
                both = [
                    jnp.where(rank_ref[source, e : e + 1, :] == slots, 1.0, 0.0)
                    for e in (2 * pair, 2 * pair + 1)
                ]
                picks[source, pair * 2 * capacity : (pair + 1) * 2 * capacity, :] = jnp.concatenate(
                    both, axis=0
                ).astype(jnp.bfloat16)

    blocks = (first_ref[...], jnp.concatenate([r[...] for r in second_refs], axis=0))
    step = 8
    for e in range(0, experts, step):
        rows = slice(e * capacity, (e + step) * capacity)
        found = [dot(picks[source, rows, :], blocks[source]) for source in range(2)]
        for i in range(step):
            own = slice(i * capacity, (i + 1) * capacity)
            out_ref[e + i] = jnp.concatenate([found[0][own], found[1][own]], axis=0).astype(
                out_ref.dtype
            )


def select(ranks, first, second, capacity, width, columns=512):
    _, experts, tok_rows = ranks.shape
    columns = min(columns, width)
    return pl.pallas_call(
        functools.partial(select_kernel, capacity=capacity),
        grid=(width // columns,),
        in_specs=[pl.BlockSpec(ranks.shape, lambda i: (0, 0, 0))]
        + [pl.BlockSpec((a.shape[0], columns), lambda i: (0, i)) for a in (first, *second)],
        out_specs=pl.BlockSpec((experts, 2 * capacity, columns), lambda i: (0, 0, i)),
        out_shape=jax.ShapeDtypeStruct((experts, 2 * capacity, width), first.dtype),
        scratch_shapes=[pltpu.VMEM((2, experts * capacity, tok_rows), jnp.bfloat16)],
        compiler_params=params(48),
        cost_estimate=pl.CostEstimate(
            flops=4 * experts * capacity * tok_rows * width, bytes_accessed=2**24, transcendentals=0
        ),
        name="select",
    )(ranks, first, *second)


def project_own_kernel(at_ref, near_ref, far_ref, factor_ref, out_ref):
    for i in range(out_ref.shape[0]):
        rows = jnp.concatenate([near_ref[i], far_ref[i]], axis=0)
        out_ref[i] = dot(rows, factor_ref[i]).astype(out_ref.dtype)


def project_kernel(at_ref, near_ref, far_ref, shared_ref, mine_ref, other_ref, out_ref):
    slices, _, _, thin, rank_k = shared_ref.shape
    half = mine_ref.shape[1]
    depth = slices * thin
    first = at_ref[1] == 0
    for i in range(out_ref.shape[0]):
        rows = jnp.concatenate([near_ref[i], far_ref[i]], axis=0)
        low, high = rows[:, depth : depth + half], rows[:, depth + half :]
        total = dot(rows[:, :depth], shared_ref[:, 0, i].reshape(depth, rank_k))
        total += dot(jnp.where(first, low, high), mine_ref[i])
        total += dot(jnp.where(first, high, low), other_ref[i])
        out_ref[i] = total.astype(out_ref.dtype)


def project(at, near, far, factors, per_group, start, count, index=None, step=2):
    width = near.shape[2]
    rank_k = factors[0].shape[-1]
    row_spec = lambda rows: pl.BlockSpec(
        (step, rows, width), lambda i, at: ((at[0] * per_group + start) // step + i, 0, 0)
    )
    plain = lambda a: pl.BlockSpec((step,) + a.shape[1:], lambda i, at: (i, 0, 0))
    if index is None:
        kernel, specs = project_own_kernel, [plain(factors[0])]
    else:
        shared = factors[0]
        kernel = project_kernel
        specs = [
            pl.BlockSpec(
                (shared.shape[0], 1, step) + shared.shape[3:],
                lambda i, at: (0, index, start // step + i, 0, 0),
            ),
            plain(factors[1]),
            plain(factors[2]),
        ]
    rows = near.shape[1] + far.shape[1]
    return pl.pallas_call(
        kernel,
        grid_spec=pltpu.PrefetchScalarGridSpec(
            num_scalar_prefetch=1,
            grid=(count // step,),
            in_specs=[row_spec(near.shape[1]), row_spec(far.shape[1])] + specs,
            out_specs=pl.BlockSpec((step, rows, rank_k), lambda i, at: (i, 0, 0)),
        ),
        out_shape=jax.ShapeDtypeStruct((count, rows, rank_k), near.dtype),
        compiler_params=params(48),
        cost_estimate=pl.CostEstimate(
            flops=2 * count * rows * width * rank_k,
            bytes_accessed=2 * count * width * (rows + rank_k),
            transcendentals=0,
        ),
        name="project",
    )(at, near, far, *factors)


def gram_kernel(at_ref, *refs, scale):
    *row_refs, mine_ref, other_ref = refs
    count, _, half, _ = mine_ref.shape
    core = at_ref[2]
    for out_ref, turn in ((mine_ref, core), (other_ref, 1 - core)):
        for i in range(count):
            rows = jnp.concatenate([r[turn * count + i] for r in row_refs], axis=0)
            lower, upper = rows[:, :half], rows[:, half:]
            transposed = ((0,), (0,))
            pairs = ((lower, lower), (lower, upper), (upper, upper))
            for block, (a, b) in enumerate(pairs):
                out_ref[i, block] = scale * lax.dot_general(
                    a, b, (transposed, ((), ())), preferred_element_type=jnp.float32
                )


def partial_grams(at, rows, scale):
    experts, _, rank_k = rows[0].shape
    half = jax.ShapeDtypeStruct((experts // 2, 3, rank_k // 2, rank_k // 2), jnp.float32)
    return pl.pallas_call(
        functools.partial(gram_kernel, scale=scale),
        in_specs=[SCALARS] + [WHOLE] * len(rows),
        out_specs=(WHOLE, WHOLE),
        out_shape=(half, half),
        compiler_params=params(16),
        name="grams",
    )(at, *rows)


def factor_kernel(at_ref, mine_ref, other_ref, *refs, block, capacity):
    *row_refs, upper_ref, codes_ref, work, high_ref, low_ref = refs
    count, _, half, _ = mine_ref.shape
    experts = 2 * count
    size = 2 * half
    lanes = 128
    groups = lanes // block
    tiles = experts // groups
    y, x, core = at_ref[0], at_ref[1], at_ref[2]
    expert = lambda e: core * count + e if e < count else (1 - core) * count + e - count
    rows_h = lax.broadcasted_iota(jnp.int32, (half, half), 0)
    cols_h = lax.broadcasted_iota(jnp.int32, (half, half), 1)
    ridge_h = jnp.where(rows_h == cols_h, RIDGE, 0.0).astype(jnp.float32)
    for e in range(experts):
        source, i = (mine_ref, e) if e < count else (other_ref, e - count)
        work[e, :half, :half] = source[i, 0] + ridge_h
        work[e, :half, half:] = source[i, 1]
        work[e, half:, half:] = source[i, 2] + ridge_h
    lane = lax.broadcasted_iota(jnp.int32, (block, lanes), 1)
    row = lax.broadcasted_iota(jnp.int32, (block, lanes), 0)
    unit = jnp.where(lane % block == row, 1.0, 0.0).astype(jnp.float32)
    base = (lane // block) * block
    for k in range(size // block):
        lo, hi = k * block, (k + 1) * block
        packed = [
            jnp.concatenate([work[t * groups + g, lo:hi, lo:hi] for g in range(groups)], axis=1)
            for t in range(tiles)
        ]
        inverse = [unit for _ in range(tiles)]
        scales = [jnp.ones((block, lanes), jnp.float32) for _ in range(tiles)]
        for j in range(0, block, 2):
            for t in range(tiles):
                s, n = packed[t], inverse[t]
                c1 = jnp.take_along_axis(s, base + j, axis=1, mode="promise_in_bounds")
                c2 = jnp.take_along_axis(s, base + (j + 1), axis=1, mode="promise_in_bounds")
                beside = c1[j + 1 : j + 2, :]
                root1 = lax.rsqrt(c1[j : j + 1, :])
                ratio = beside * (root1 * root1)
                root2 = lax.rsqrt(c2[j + 1 : j + 2, :] - ratio * beside)
                scales[t] = jnp.where(row == j, root1, jnp.where(row == j + 1, root2, scales[t]))
                f1 = jnp.where(row > j, c1 * (root1 * root1), 0.0)
                f2 = jnp.where(row > j + 1, (c2 - c1 * ratio) * (root2 * root2), 0.0)
                s1, s2 = s[j : j + 1, :], s[j + 1 : j + 2, :]
                n1, n2 = n[j : j + 1, :], n[j + 1 : j + 2, :]
                packed[t] = s - f1 * s1 - f2 * (s2 - ratio * s1)
                inverse[t] = n - f1 * n1 - f2 * (n2 - ratio * n1)
        packed = [jnp.where(lane % block >= row, s * c, 0.0) for s, c in zip(packed, scales)]
        inverse = [n * c for n, c in zip(inverse, scales)]
        for e in range(experts):
            t, g = e // groups, e % groups
            own = expert(e)
            work[e, lo:hi, lo:hi] = jnp.eye(block, dtype=jnp.float32)
            strip = exact_dot(
                inverse[t][:, g * block : (g + 1) * block], work[e, lo:hi, :], ((1,), (0,))
            )
            if lo:
                upper_ref[own, lo:hi, :lo] = jnp.zeros((block, lo), jnp.float32)
            upper_ref[own, lo:hi, lo:hi] = packed[t][:, g * block : (g + 1) * block]
            work[e, lo:hi, :] = strip
            if hi < size:
                upper_ref[own, lo:hi, hi:] = strip[:, hi:]
                work[e, hi:, lo:hi] = jnp.zeros((size - hi, block), jnp.float32)
                work[e, hi:, :] = work[e, hi:, :] - exact_dot(strip[:, hi:], strip, ((0,), (0,)))
    rows = lax.broadcasted_iota(jnp.int32, (size, size), 0)
    cols = lax.broadcasted_iota(jnp.int32, (size, size), 1)
    for e in range(experts):
        whole = jnp.where(rows >= cols, work[e], 0.0)
        high = whole.astype(jnp.bfloat16)
        high_ref[expert(e)] = high
        low_ref[expert(e)] = (whole - high.astype(jnp.float32)).astype(jnp.bfloat16)

    across = (((1,), (1,)), ((), ()))
    for away, rows_ref in zip((0, 1, -1, 2), row_refs):
        found = []
        for e in range(experts):
            a = rows_ref[e]
            found.append(
                lax.dot_general(a, high_ref[e], across, preferred_element_type=jnp.float32)
                + lax.dot_general(a, low_ref[e], across, preferred_element_type=jnp.float32)
            )
        for i, step in enumerate(NEAR):
            owner = lax.rem(y + step + SIDE, SIDE) * SIDE + lax.rem(x + away + SIDE, SIDE)
            own = slice(i * capacity, (i + 1) * capacity)
            codes_ref[owner] = jnp.concatenate([f[own] for f in found], axis=0).astype(
                codes_ref.dtype
            )


def factorize(at, mine, other, rows, capacity):
    count, _, half, _ = mine.shape
    experts, size = 2 * count, 2 * half
    square = (experts, size, size)
    return pl.pallas_call(
        functools.partial(factor_kernel, block=BLOCK, capacity=capacity),
        in_specs=[SCALARS] + [WHOLE] * (2 + len(rows)),
        out_specs=(WHOLE, WHOLE),
        out_shape=(
            jax.ShapeDtypeStruct(square, jnp.float32),
            jax.ShapeDtypeStruct((SIDE * SIDE, experts * capacity, size), jnp.bfloat16),
        ),
        scratch_shapes=[
            pltpu.VMEM(square, jnp.float32),
            pltpu.VMEM(square, jnp.bfloat16),
            pltpu.VMEM(square, jnp.bfloat16),
        ],
        compiler_params=params(24),
        name="factorize",
    )(at, mine, other, *rows)


def slot_ranks(ids, first, experts):
    blocks, rows, _ = ids.shape
    wanted = first + jnp.arange(experts, dtype=jnp.int32)
    named = (jnp.swapaxes(ids, 1, 2)[:, :, None, :] == wanted[None, None, :, None]).any(axis=1)
    later = jnp.arange(rows)[:, None] < jnp.arange(rows)[None, :]
    rank = dot(named.reshape(-1, rows).astype(jnp.bfloat16), later.astype(jnp.bfloat16))
    return jnp.where(named, rank.reshape(named.shape), -1.0)


def sum_over_tok(mine, other):
    shape = mine.shape
    lanes = shape[-1]
    layers = lax.axis_size("z")
    mine = mine + shift(other, "c", 1)
    pieces = lax.all_to_all(mine.reshape(layers, -1, lanes), "z", 0, 0, tiled=True)
    mine = lax.all_gather(jnp.sum(pieces, axis=0), "z", tiled=True)
    other = shift(mine, "c", 1)
    return mine.reshape(shape), other.reshape(shape)


def local(tokens, first_factor, expert_ids):
    groups = lax.axis_size(("y", "x"))
    tok_ranks = lax.axis_size(("z", "c"))
    per_group, model_dim, rank_k = first_factor.shape
    tok_rows, top_k = expert_ids.shape
    experts = groups * per_group
    capacity = tok_rows * top_k * 5 // (4 * experts)
    gram_scale = experts / (top_k * tok_rows * tok_ranks * groups)
    y, x, core = lax.axis_index("y"), lax.axis_index("x"), lax.axis_index("c")
    at = jnp.stack([y, x, core]).astype(jnp.int32)

    depth = model_dim // 2
    thin = depth // tok_ranks
    thick = depth // 2
    middle = per_group // 2
    half_rows = tok_rows // 2
    tied = lax.optimization_barrier
    lanes = 128
    tagged = jnp.concatenate(
        [tokens, jnp.pad(expert_ids.astype(tokens.dtype), ((0, 0), (0, lanes - top_k)))], axis=1
    )
    slices = lax.dynamic_slice_in_dim(first_factor, lax.axis_index(("z", "c")) * thin, thin, 1)
    thick_slice = lax.dynamic_slice_in_dim(first_factor, depth + core * thick, thick, 1)
    slices_before, slices_after, slices_far = shift(slices, "x", 1), shift(slices, "x", -1), shift(slices, "x", 2)
    tagged, thick_slice, slices_before, slices_after, slices_far = tied(
        (tagged, thick_slice, slices_before, slices_after, slices_far)
    )
    shared = lax.all_gather(jnp.stack([slices_before, slices_after, slices_far]), ("z", "c"))
    tokens_before, tokens_after, mine_before, mine_after = tied(
        (
            shift(tagged, "y", 1),
            shift(tagged, "y", -1),
            shift(thick_slice, "x", 1),
            shift(thick_slice, "x", -1),
        )
    )
    tokens_far = [shift(tokens_before[:half_rows], "y", 1), shift(tokens_after[half_rows:], "y", -1)]
    mine_far = [shift(mine_before[:middle], "x", 1), shift(mine_after[middle:], "x", -1)]
    ids_of = lambda a: a[:, model_dim : model_dim + top_k].astype(jnp.int32)
    first_of = y * SIDE * per_group
    near_ids = jnp.stack([expert_ids, ids_of(tokens_before)])
    near = select(
        slot_ranks(near_ids, first_of, SIDE * per_group),
        tokens,
        [tokens_before],
        capacity,
        model_dim,
    )
    near, mine_before, mine_after, *arrived = tied(
        (near, mine_before, mine_after, *tokens_far, *mine_far)
    )
    tokens_far, mine_far = arrived[:2], arrived[2:]
    far_ids = jnp.stack(
        [ids_of(tokens_after), jnp.concatenate([ids_of(a) for a in tokens_far], axis=0)]
    )
    far = select(
        slot_ranks(far_ids, first_of, SIDE * per_group),
        tokens_after,
        tokens_far,
        capacity,
        model_dim,
    )
    swap = lambda a: (a, shift(a, "c", 1))

    def projected(step, factors, start, count, index=None):
        where = jnp.stack([(x + step) % SIDE, core]).astype(jnp.int32)
        return project(where, near, far, factors, per_group, start, count, index)

    to_far = [
        projected(2, [shared, *swap(mine_far[i])], i * middle, middle, 2) for i in range(2)
    ]
    near, far, *to_far = tied((near, far, *to_far))
    from_after = shift(projected(-1, [shared, *swap(mine_before)], 0, per_group, 0), "x", -1)
    from_before = shift(projected(1, [shared, *swap(mine_after)], 0, per_group, 1), "x", 1)
    rows_own = projected(0, [first_factor], 0, per_group)
    from_far = jnp.concatenate([shift(a, "x", 2) for a in to_far], axis=0)
    rows_own, expert_ids = tied((rows_own, expert_ids))
    rows = [rows_own, from_after, from_before, from_far]

    mine, other = sum_over_tok(*partial_grams(at, rows, gram_scale))
    upper, codes = factorize(at, mine, other, rows, capacity)
    returned = lax.all_to_all(codes, ("y", "x"), 0, 0, tiled=True)

    own_ranks = slot_ranks(expert_ids[None], 0, experts)[0]
    named = expert_ids.T[:, None, :] == jnp.arange(experts, dtype=jnp.int32)[None, :, None]
    slot = expert_ids.T * capacity + jnp.sum(jnp.where(named, own_ranks, 0.0), axis=1).astype(jnp.int32)
    gathered = returned.reshape(experts * capacity, rank_k)[slot.T.reshape(-1)]
    return (gathered.reshape(tok_rows, top_k, rank_k), upper)


def solution(mesh):
    fine = Mesh(mesh.devices.reshape(-1, 2, SIDE, SIDE), ("z", "c", "y", "x"))
    every = ("z", "c", "y", "x")
    in_specs = (P(every, None), P(("y", "x"), None, None), P(every, None))
    out_specs = (P(every, None, None), P(("y", "x"), None, None))
    return jax.shard_map(local, mesh=fine, in_specs=in_specs, out_specs=out_specs, check_vma=False)
```

```python
import functools

import jax
import jax.numpy as jnp
from jax import lax
from jax.experimental import pallas as pl
from jax.experimental.pallas import tpu as pltpu
from jax.sharding import Mesh
from jax.sharding import PartitionSpec as P

RIDGE = 0.1
BLOCK = 32
SIDE = 4
NEAR = (0, -1, 1, 2)
WHOLE = pl.BlockSpec(memory_space=pltpu.VMEM)
SCALARS = pl.BlockSpec(memory_space=pltpu.SMEM)


def params(mebibytes):
    return pltpu.CompilerParams(vmem_limit_bytes=mebibytes * 2**20)


def exact_dot(a, b, dims):
    return lax.dot_general(
        a, b, (dims, ((), ())), precision=lax.Precision.HIGHEST, preferred_element_type=jnp.float32
    )


def dot(a, b):
    return jnp.dot(a, b, preferred_element_type=jnp.float32)


def shift(array, axis, step):
    size = lax.axis_size(axis)
    return lax.ppermute(array, axis, [(i, (i + step) % size) for i in range(size)])


def select_kernel(rank_ref, first_ref, *rest, capacity):
    *second_refs, out_ref, picks = rest
    experts, tok_rows = rank_ref.shape[1:]

    @pl.when(pl.program_id(0) == 0)
    def _():
        slots = lax.broadcasted_iota(jnp.int32, (capacity, tok_rows), 0).astype(jnp.float32)
        for source in range(2):
            for pair in range(experts // 2):
                both = [
                    jnp.where(rank_ref[source, e : e + 1, :] == slots, 1.0, 0.0)
                    for e in (2 * pair, 2 * pair + 1)
                ]
                picks[source, pair * 2 * capacity : (pair + 1) * 2 * capacity, :] = jnp.concatenate(
                    both, axis=0
                ).astype(jnp.bfloat16)

    blocks = (first_ref[...], jnp.concatenate([r[...] for r in second_refs], axis=0))
    step = 8
    for e in range(0, experts, step):
        rows = slice(e * capacity, (e + step) * capacity)
        found = [dot(picks[source, rows, :], blocks[source]) for source in range(2)]
        for i in range(step):
            own = slice(i * capacity, (i + 1) * capacity)
            out_ref[e + i] = jnp.concatenate([found[0][own], found[1][own]], axis=0).astype(
                out_ref.dtype
            )


def select(ranks, first, second, capacity, width, columns=512):
    _, experts, tok_rows = ranks.shape
    columns = min(columns, width)
    return pl.pallas_call(
        functools.partial(select_kernel, capacity=capacity),
        grid=(width // columns,),
        in_specs=[pl.BlockSpec(ranks.shape, lambda i: (0, 0, 0))]
        + [pl.BlockSpec((a.shape[0], columns), lambda i: (0, i)) for a in (first, *second)],
        out_specs=pl.BlockSpec((experts, 2 * capacity, columns), lambda i: (0, 0, i)),
        out_shape=jax.ShapeDtypeStruct((experts, 2 * capacity, width), first.dtype),
        scratch_shapes=[pltpu.VMEM((2, experts * capacity, tok_rows), jnp.bfloat16)],
        compiler_params=params(48),
        cost_estimate=pl.CostEstimate(
            flops=4 * experts * capacity * tok_rows * width, bytes_accessed=2**24, transcendentals=0
        ),
        name="select",
    )(ranks, first, *second)


def project_own_kernel(at_ref, near_ref, far_ref, factor_ref, out_ref):
    for i in range(out_ref.shape[0]):
        rows = jnp.concatenate([near_ref[i], far_ref[i]], axis=0)
        out_ref[i] = dot(rows, factor_ref[i]).astype(out_ref.dtype)


def project_kernel(at_ref, near_ref, far_ref, shared_ref, mine_ref, other_ref, out_ref):
    slices, _, _, thin, rank_k = shared_ref.shape
    half = mine_ref.shape[1]
    depth = slices * thin
    first = at_ref[1] == 0
    for i in range(out_ref.shape[0]):
        rows = jnp.concatenate([near_ref[i], far_ref[i]], axis=0)
        low, high = rows[:, depth : depth + half], rows[:, depth + half :]
        total = dot(rows[:, :depth], shared_ref[:, 0, i].reshape(depth, rank_k))
        total += dot(jnp.where(first, low, high), mine_ref[i])
        total += dot(jnp.where(first, high, low), other_ref[i])
        out_ref[i] = total.astype(out_ref.dtype)


def project(at, near, far, factors, per_group, start, count, index=None, step=2):
    width = near.shape[2]
    rank_k = factors[0].shape[-1]
    row_spec = lambda rows: pl.BlockSpec(
        (step, rows, width), lambda i, at: ((at[0] * per_group + start) // step + i, 0, 0)
    )
    plain = lambda a: pl.BlockSpec((step,) + a.shape[1:], lambda i, at: (i, 0, 0))
    if index is None:
        kernel, specs = project_own_kernel, [plain(factors[0])]
    else:
        shared = factors[0]
        kernel = project_kernel
        specs = [
            pl.BlockSpec(
                (shared.shape[0], 1, step) + shared.shape[3:],
                lambda i, at: (0, index, start // step + i, 0, 0),
            ),
            plain(factors[1]),
            plain(factors[2]),
        ]
    rows = near.shape[1] + far.shape[1]
    return pl.pallas_call(
        kernel,
        grid_spec=pltpu.PrefetchScalarGridSpec(
            num_scalar_prefetch=1,
            grid=(count // step,),
            in_specs=[row_spec(near.shape[1]), row_spec(far.shape[1])] + specs,
            out_specs=pl.BlockSpec((step, rows, rank_k), lambda i, at: (i, 0, 0)),
        ),
        out_shape=jax.ShapeDtypeStruct((count, rows, rank_k), near.dtype),
        compiler_params=params(48),
        cost_estimate=pl.CostEstimate(
            flops=2 * count * rows * width * rank_k,
            bytes_accessed=2 * count * width * (rows + rank_k),
            transcendentals=0,
        ),
        name="project",
    )(at, near, far, *factors)


def gram_kernel(at_ref, *refs, scale):
    *row_refs, mine_ref, other_ref = refs
    count, _, half, _ = mine_ref.shape
    core = at_ref[2]
    for out_ref, turn in ((mine_ref, core), (other_ref, 1 - core)):
        for i in range(count):
            rows = jnp.concatenate([r[turn * count + i] for r in row_refs], axis=0)
            lower, upper = rows[:, :half], rows[:, half:]
            transposed = ((0,), (0,))
            pairs = ((lower, lower), (lower, upper), (upper, upper))
            for block, (a, b) in enumerate(pairs):
                out_ref[i, block] = scale * lax.dot_general(
                    a, b, (transposed, ((), ())), preferred_element_type=jnp.float32
                )


def partial_grams(at, rows, scale):
    experts, _, rank_k = rows[0].shape
    half = jax.ShapeDtypeStruct((experts // 2, 3, rank_k // 2, rank_k // 2), jnp.float32)
    return pl.pallas_call(
        functools.partial(gram_kernel, scale=scale),
        in_specs=[SCALARS] + [WHOLE] * len(rows),
        out_specs=(WHOLE, WHOLE),
        out_shape=(half, half),
        compiler_params=params(16),
        name="grams",
    )(at, *rows)


def factor_kernel(gram_ref, upper_ref, inverse_ref, work, *, block):
    experts, _, half, _ = gram_ref.shape
    size = 2 * half
    lanes = 128
    groups = lanes // block
    tiles = experts // groups
    rows_h = lax.broadcasted_iota(jnp.int32, (half, half), 0)
    cols_h = lax.broadcasted_iota(jnp.int32, (half, half), 1)
    ridge_h = jnp.where(rows_h == cols_h, RIDGE, 0.0).astype(jnp.float32)
    for e in range(experts):
        work[e, :half, :half] = gram_ref[e, 0] + ridge_h
        work[e, :half, half:] = gram_ref[e, 1]
        work[e, half:, half:] = gram_ref[e, 2] + ridge_h
    lane = lax.broadcasted_iota(jnp.int32, (block, lanes), 1)
    row = lax.broadcasted_iota(jnp.int32, (block, lanes), 0)
    unit = jnp.where(lane % block == row, 1.0, 0.0).astype(jnp.float32)
    base = (lane // block) * block
    for k in range(size // block):
        lo, hi = k * block, (k + 1) * block
        packed = [
            jnp.concatenate([work[t * groups + g, lo:hi, lo:hi] for g in range(groups)], axis=1)
            for t in range(tiles)
        ]
        inverse = [unit for _ in range(tiles)]
        scales = [jnp.ones((block, lanes), jnp.float32) for _ in range(tiles)]
        for j in range(0, block, 2):
            for t in range(tiles):
                s, n = packed[t], inverse[t]
                c1 = jnp.take_along_axis(s, base + j, axis=1, mode="promise_in_bounds")
                c2 = jnp.take_along_axis(s, base + (j + 1), axis=1, mode="promise_in_bounds")
                beside = c1[j + 1 : j + 2, :]
                root1 = lax.rsqrt(c1[j : j + 1, :])
                ratio = beside * (root1 * root1)
                root2 = lax.rsqrt(c2[j + 1 : j + 2, :] - ratio * beside)
                scales[t] = jnp.where(row == j, root1, jnp.where(row == j + 1, root2, scales[t]))
                f1 = jnp.where(row > j, c1 * (root1 * root1), 0.0)
                f2 = jnp.where(row > j + 1, (c2 - c1 * ratio) * (root2 * root2), 0.0)
                s1, s2 = s[j : j + 1, :], s[j + 1 : j + 2, :]
                n1, n2 = n[j : j + 1, :], n[j + 1 : j + 2, :]
                packed[t] = s - f1 * s1 - f2 * (s2 - ratio * s1)
                inverse[t] = n - f1 * n1 - f2 * (n2 - ratio * n1)
        packed = [jnp.where(lane % block >= row, s * c, 0.0) for s, c in zip(packed, scales)]
        inverse = [n * c for n, c in zip(inverse, scales)]
        for e in range(experts):
            t, g = e // groups, e % groups
            work[e, lo:hi, lo:hi] = jnp.eye(block, dtype=jnp.float32)
            strip = exact_dot(
                inverse[t][:, g * block : (g + 1) * block], work[e, lo:hi, :], ((1,), (0,))
            )
            if lo:
                upper_ref[e, lo:hi, :lo] = jnp.zeros((block, lo), jnp.float32)
            upper_ref[e, lo:hi, lo:hi] = packed[t][:, g * block : (g + 1) * block]
            work[e, lo:hi, :] = strip
            if hi < size:
                upper_ref[e, lo:hi, hi:] = strip[:, hi:]
                work[e, hi:, lo:hi] = jnp.zeros((size - hi, block), jnp.float32)
                work[e, hi:, :] = work[e, hi:, :] - exact_dot(strip[:, hi:], strip, ((0,), (0,)))
    rows = lax.broadcasted_iota(jnp.int32, (size, size), 0)
    cols = lax.broadcasted_iota(jnp.int32, (size, size), 1)
    for e in range(experts):
        whole = jnp.where(rows >= cols, work[e], 0.0)
        high = whole.astype(jnp.bfloat16)
        inverse_ref[0, e] = high
        inverse_ref[1, e] = (whole - high.astype(jnp.float32)).astype(jnp.bfloat16)


def factorize(grams):
    experts, _, half, _ = grams.shape
    square = (experts, 2 * half, 2 * half)
    return pl.pallas_call(
        functools.partial(factor_kernel, block=BLOCK),
        in_specs=[WHOLE],
        out_specs=(WHOLE, WHOLE),
        out_shape=(
            jax.ShapeDtypeStruct(square, jnp.float32),
            jax.ShapeDtypeStruct((2,) + square, jnp.bfloat16),
        ),
        scratch_shapes=[pltpu.VMEM(square, jnp.float32)],
        compiler_params=params(24),
        name="factorize",
    )(grams)


def whiten_kernel(at_ref, mine_ref, other_ref, *refs, capacity):
    *row_refs, codes_ref = refs
    count = mine_ref.shape[1]
    y, x, core = at_ref[0], at_ref[1], at_ref[2]
    across = (((1,), (1,)), ((), ()))
    terms = [
        [
            jnp.where(core == e // count, mine_ref[term, e % count], other_ref[term, e % count])
            for term in range(2)
        ]
        for e in range(2 * count)
    ]
    for away, rows_ref in zip((0, 1, -1, 2), row_refs):
        found = [
            sum(
                lax.dot_general(rows_ref[e], term, across, preferred_element_type=jnp.float32)
                for term in terms[e]
            )
            for e in range(2 * count)
        ]
        for i, step in enumerate(NEAR):
            owner = lax.rem(y + step + SIDE, SIDE) * SIDE + lax.rem(x + away + SIDE, SIDE)
            own = slice(i * capacity, (i + 1) * capacity)
            codes_ref[owner] = jnp.concatenate([f[own] for f in found], axis=0).astype(
                codes_ref.dtype
            )


def whiten(at, mine, other, rows, capacity):
    _, count, size, _ = mine.shape
    return pl.pallas_call(
        functools.partial(whiten_kernel, capacity=capacity),
        in_specs=[SCALARS] + [WHOLE] * (2 + len(rows)),
        out_specs=WHOLE,
        out_shape=jax.ShapeDtypeStruct((SIDE * SIDE, 2 * count * capacity, size), jnp.bfloat16),
        compiler_params=params(24),
        name="whiten",
    )(at, mine, other, *rows)


def slot_ranks(ids, first, experts):
    blocks, rows, _ = ids.shape
    wanted = first + jnp.arange(experts, dtype=jnp.int32)
    named = (jnp.swapaxes(ids, 1, 2)[:, :, None, :] == wanted[None, None, :, None]).any(axis=1)
    later = jnp.arange(rows)[:, None] < jnp.arange(rows)[None, :]
    rank = dot(named.reshape(-1, rows).astype(jnp.bfloat16), later.astype(jnp.bfloat16))
    return jnp.where(named, rank.reshape(named.shape), -1.0)


def sum_over_tok(mine, other):
    shape = mine.shape
    lanes = shape[-1]
    layers = lax.axis_size("z")
    mine = mine + shift(other, "c", 1)
    pieces = lax.all_to_all(mine.reshape(layers, -1, lanes), "z", 0, 0, tiled=True)
    return lax.all_gather(jnp.sum(pieces, axis=0), "z", tiled=True).reshape(shape)


def local(tokens, first_factor, expert_ids):
    groups = lax.axis_size(("y", "x"))
    tok_ranks = lax.axis_size(("z", "c"))
    per_group, model_dim, rank_k = first_factor.shape
    tok_rows, top_k = expert_ids.shape
    experts = groups * per_group
    capacity = tok_rows * top_k * 5 // (4 * experts)
    gram_scale = experts / (top_k * tok_rows * tok_ranks * groups)
    y, x, core = lax.axis_index("y"), lax.axis_index("x"), lax.axis_index("c")
    at = jnp.stack([y, x, core]).astype(jnp.int32)

    depth = model_dim // 2
    thin = depth // tok_ranks
    thick = depth // 2
    middle = per_group // 2
    half_rows = tok_rows // 2
    tied = lax.optimization_barrier
    lanes = 128
    tagged = jnp.concatenate(
        [tokens, jnp.pad(expert_ids.astype(tokens.dtype), ((0, 0), (0, lanes - top_k)))], axis=1
    )
    slices = lax.dynamic_slice_in_dim(first_factor, lax.axis_index(("z", "c")) * thin, thin, 1)
    thick_slice = lax.dynamic_slice_in_dim(first_factor, depth + core * thick, thick, 1)
    slices_before, slices_after, slices_far = shift(slices, "x", 1), shift(slices, "x", -1), shift(slices, "x", 2)
    tagged, thick_slice, slices_before, slices_after, slices_far = tied(
        (tagged, thick_slice, slices_before, slices_after, slices_far)
    )
    shared = lax.all_gather(jnp.stack([slices_before, slices_after, slices_far]), ("z", "c"))
    tokens_before, tokens_after, mine_before, mine_after = tied(
        (
            shift(tagged, "y", 1),
            shift(tagged, "y", -1),
            shift(thick_slice, "x", 1),
            shift(thick_slice, "x", -1),
        )
    )
    tokens_far = [shift(tokens_before[:half_rows], "y", 1), shift(tokens_after[half_rows:], "y", -1)]
    mine_far = [shift(mine_before[:middle], "x", 1), shift(mine_after[middle:], "x", -1)]
    ids_of = lambda a: a[:, model_dim : model_dim + top_k].astype(jnp.int32)
    first_of = y * SIDE * per_group
    near_ids = jnp.stack([expert_ids, ids_of(tokens_before)])
    near = select(
        slot_ranks(near_ids, first_of, SIDE * per_group),
        tokens,
        [tokens_before],
        capacity,
        model_dim,
    )
    near, *tokens_far = tied((near, *tokens_far))
    far_ids = jnp.stack(
        [ids_of(tokens_after), jnp.concatenate([ids_of(a) for a in tokens_far], axis=0)]
    )
    far = select(
        slot_ranks(far_ids, first_of, SIDE * per_group),
        tokens_after,
        tokens_far,
        capacity,
        model_dim,
    )
    far, mine_before, mine_after, *mine_far = tied((far, mine_before, mine_after, *mine_far))
    swap = lambda a: (a, shift(a, "c", 1))

    def projected(step, factors, start, count, index=None):
        where = jnp.stack([(x + step) % SIDE, core]).astype(jnp.int32)
        return project(where, near, far, factors, per_group, start, count, index)

    to_far = [
        projected(2, [shared, *swap(mine_far[i])], i * middle, middle, 2) for i in range(2)
    ]
    near, far, *to_far = tied((near, far, *to_far))
    from_after = shift(projected(-1, [shared, *swap(mine_before)], 0, per_group, 0), "x", -1)
    from_before = shift(projected(1, [shared, *swap(mine_after)], 0, per_group, 1), "x", 1)
    rows_own = projected(0, [first_factor], 0, per_group)
    from_far = jnp.concatenate([shift(a, "x", 2) for a in to_far], axis=0)
    rows_own, expert_ids = tied((rows_own, expert_ids))
    rows = [rows_own, from_after, from_before, from_far]

    upper, inverse = factorize(sum_over_tok(*partial_grams(at, rows, gram_scale)))
    codes = whiten(at, inverse, shift(inverse, "c", 1), rows, capacity)
    upper, codes = tied((upper, codes))
    returned = lax.all_to_all(codes, ("y", "x"), 0, 0, tiled=True)
    other = shift(upper, "c", 1)
    upper = jnp.where(
        core == 0, jnp.concatenate([upper, other]), jnp.concatenate([other, upper])
    )

    own_ranks = slot_ranks(expert_ids[None], 0, experts)[0]
    named = expert_ids.T[:, None, :] == jnp.arange(experts, dtype=jnp.int32)[None, :, None]
    slot = expert_ids.T * capacity + jnp.sum(jnp.where(named, own_ranks, 0.0), axis=1).astype(jnp.int32)
    gathered = returned.reshape(experts * capacity, rank_k)[slot.T.reshape(-1)]
    return (gathered.reshape(tok_rows, top_k, rank_k), upper)


def solution(mesh):
    fine = Mesh(mesh.devices.reshape(-1, 2, SIDE, SIDE), ("z", "c", "y", "x"))
    every = ("z", "c", "y", "x")
    in_specs = (P(every, None), P(("y", "x"), None, None), P(every, None))
    out_specs = (P(every, None, None), P(("y", "x"), None, None))
    return jax.shard_map(local, mesh=fine, in_specs=in_specs, out_specs=out_specs, check_vma=False)
```

```python
import functools

import jax
import jax.numpy as jnp
from jax import lax
from jax.experimental import pallas as pl
from jax.experimental.pallas import tpu as pltpu
from jax.sharding import Mesh
from jax.sharding import PartitionSpec as P

RIDGE = 0.1
BLOCK = 32
SIDE = 4
NEAR = (0, -1, 1, 2)
WHOLE = pl.BlockSpec(memory_space=pltpu.VMEM)
SCALARS = pl.BlockSpec(memory_space=pltpu.SMEM)


def params(mebibytes):
    return pltpu.CompilerParams(vmem_limit_bytes=mebibytes * 2**20)


def exact_dot(a, b, dims):
    return lax.dot_general(
        a, b, (dims, ((), ())), precision=lax.Precision.HIGHEST, preferred_element_type=jnp.float32
    )


def dot(a, b):
    return jnp.dot(a, b, preferred_element_type=jnp.float32)


def shift(array, axis, step):
    size = lax.axis_size(axis)
    return lax.ppermute(array, axis, [(i, (i + step) % size) for i in range(size)])


def select_kernel(rank_ref, first_ref, *rest, capacity):
    *second_refs, out_ref, picks = rest
    experts, tok_rows = rank_ref.shape[1:]

    @pl.when(pl.program_id(0) == 0)
    def _():
        slots = lax.broadcasted_iota(jnp.int32, (capacity, tok_rows), 0).astype(jnp.float32)
        for source in range(2):
            for pair in range(experts // 2):
                both = [
                    jnp.where(rank_ref[source, e : e + 1, :] == slots, 1.0, 0.0)
                    for e in (2 * pair, 2 * pair + 1)
                ]
                picks[source, pair * 2 * capacity : (pair + 1) * 2 * capacity, :] = jnp.concatenate(
                    both, axis=0
                ).astype(jnp.bfloat16)

    blocks = (first_ref[...], jnp.concatenate([r[...] for r in second_refs], axis=0))
    step = 8
    for e in range(0, experts, step):
        rows = slice(e * capacity, (e + step) * capacity)
        found = [dot(picks[source, rows, :], blocks[source]) for source in range(2)]
        for i in range(step):
            own = slice(i * capacity, (i + 1) * capacity)
            out_ref[e + i] = jnp.concatenate([found[0][own], found[1][own]], axis=0).astype(
                out_ref.dtype
            )


def select(ranks, first, second, capacity, width, columns=512):
    _, experts, tok_rows = ranks.shape
    columns = min(columns, width)
    return pl.pallas_call(
        functools.partial(select_kernel, capacity=capacity),
        grid=(width // columns,),
        in_specs=[pl.BlockSpec(ranks.shape, lambda i: (0, 0, 0))]
        + [pl.BlockSpec((a.shape[0], columns), lambda i: (0, i)) for a in (first, *second)],
        out_specs=pl.BlockSpec((experts, 2 * capacity, columns), lambda i: (0, 0, i)),
        out_shape=jax.ShapeDtypeStruct((experts, 2 * capacity, width), first.dtype),
        scratch_shapes=[pltpu.VMEM((2, experts * capacity, tok_rows), jnp.bfloat16)],
        compiler_params=params(48),
        cost_estimate=pl.CostEstimate(
            flops=4 * experts * capacity * tok_rows * width, bytes_accessed=2**24, transcendentals=0
        ),
        name="select",
    )(ranks, first, *second)


def project_own_kernel(at_ref, near_ref, far_ref, factor_ref, out_ref):
    for i in range(out_ref.shape[0]):
        rows = jnp.concatenate([near_ref[i], far_ref[i]], axis=0)
        out_ref[i] = dot(rows, factor_ref[i]).astype(out_ref.dtype)


def project_kernel(at_ref, near_ref, far_ref, shared_ref, mine_ref, other_ref, out_ref):
    slices, _, _, thin, rank_k = shared_ref.shape
    half = mine_ref.shape[1]
    depth = slices * thin
    first = at_ref[1] == 0
    for i in range(out_ref.shape[0]):
        rows = jnp.concatenate([near_ref[i], far_ref[i]], axis=0)
        low, high = rows[:, depth : depth + half], rows[:, depth + half :]
        total = dot(rows[:, :depth], shared_ref[:, 0, i].reshape(depth, rank_k))
        total += dot(jnp.where(first, low, high), mine_ref[i])
        total += dot(jnp.where(first, high, low), other_ref[i])
        out_ref[i] = total.astype(out_ref.dtype)


def project(at, near, far, factors, per_group, start, count, index=None, step=2):
    width = near.shape[2]
    rank_k = factors[0].shape[-1]
    row_spec = lambda rows: pl.BlockSpec(
        (step, rows, width), lambda i, at: ((at[0] * per_group + start) // step + i, 0, 0)
    )
    plain = lambda a: pl.BlockSpec((step,) + a.shape[1:], lambda i, at: (i, 0, 0))
    if index is None:
        kernel, specs = project_own_kernel, [plain(factors[0])]
    else:
        shared = factors[0]
        kernel = project_kernel
        specs = [
            pl.BlockSpec(
                (shared.shape[0], 1, step) + shared.shape[3:],
                lambda i, at: (0, index, start // step + i, 0, 0),
            ),
            plain(factors[1]),
            plain(factors[2]),
        ]
    rows = near.shape[1] + far.shape[1]
    return pl.pallas_call(
        kernel,
        grid_spec=pltpu.PrefetchScalarGridSpec(
            num_scalar_prefetch=1,
            grid=(count // step,),
            in_specs=[row_spec(near.shape[1]), row_spec(far.shape[1])] + specs,
            out_specs=pl.BlockSpec((step, rows, rank_k), lambda i, at: (i, 0, 0)),
        ),
        out_shape=jax.ShapeDtypeStruct((count, rows, rank_k), near.dtype),
        compiler_params=params(48),
        cost_estimate=pl.CostEstimate(
            flops=2 * count * rows * width * rank_k,
            bytes_accessed=2 * count * width * (rows + rank_k),
            transcendentals=0,
        ),
        name="project",
    )(at, near, far, *factors)


def gram_kernel(at_ref, *refs, scale):
    *row_refs, mine_ref, other_ref = refs
    count, _, half, _ = mine_ref.shape
    core = at_ref[2]
    for out_ref, turn in ((mine_ref, core), (other_ref, 1 - core)):
        for i in range(count):
            rows = jnp.concatenate([r[turn * count + i] for r in row_refs], axis=0)
            lower, upper = rows[:, :half], rows[:, half:]
            transposed = ((0,), (0,))
            pairs = ((lower, lower), (lower, upper), (upper, upper))
            for block, (a, b) in enumerate(pairs):
                out_ref[i, block] = scale * lax.dot_general(
                    a, b, (transposed, ((), ())), preferred_element_type=jnp.float32
                )


def partial_grams(at, rows, scale):
    experts, _, rank_k = rows[0].shape
    half = jax.ShapeDtypeStruct((experts // 2, 3, rank_k // 2, rank_k // 2), jnp.float32)
    return pl.pallas_call(
        functools.partial(gram_kernel, scale=scale),
        in_specs=[SCALARS] + [WHOLE] * len(rows),
        out_specs=(WHOLE, WHOLE),
        out_shape=(half, half),
        compiler_params=params(16),
        name="grams",
    )(at, *rows)


def factor_kernel(gram_ref, upper_ref, inverse_ref, work, *, block):
    experts, _, half, _ = gram_ref.shape
    size = 2 * half
    lanes = 128
    groups = lanes // block
    tiles = experts // groups
    rows_h = lax.broadcasted_iota(jnp.int32, (half, half), 0)
    cols_h = lax.broadcasted_iota(jnp.int32, (half, half), 1)
    ridge_h = jnp.where(rows_h == cols_h, RIDGE, 0.0).astype(jnp.float32)
    for e in range(experts):
        work[e, :half, :half] = gram_ref[e, 0] + ridge_h
        work[e, :half, half:] = gram_ref[e, 1]
        work[e, half:, half:] = gram_ref[e, 2] + ridge_h
    lane = lax.broadcasted_iota(jnp.int32, (block, lanes), 1)
    row = lax.broadcasted_iota(jnp.int32, (block, lanes), 0)
    unit = jnp.where(lane % block == row, 1.0, 0.0).astype(jnp.float32)
    base = (lane // block) * block
    for k in range(size // block):
        lo, hi = k * block, (k + 1) * block
        packed = [
            jnp.concatenate([work[t * groups + g, lo:hi, lo:hi] for g in range(groups)], axis=1)
            for t in range(tiles)
        ]
        inverse = [unit for _ in range(tiles)]
        scales = [jnp.ones((block, lanes), jnp.float32) for _ in range(tiles)]
        for j in range(0, block, 2):
            for t in range(tiles):
                s, n = packed[t], inverse[t]
                c1 = jnp.take_along_axis(s, base + j, axis=1, mode="promise_in_bounds")
                c2 = jnp.take_along_axis(s, base + (j + 1), axis=1, mode="promise_in_bounds")
                beside = c1[j + 1 : j + 2, :]
                root1 = lax.rsqrt(c1[j : j + 1, :])
                ratio = beside * (root1 * root1)
                root2 = lax.rsqrt(c2[j + 1 : j + 2, :] - ratio * beside)
                scales[t] = jnp.where(row == j, root1, jnp.where(row == j + 1, root2, scales[t]))
                f1 = jnp.where(row > j, c1 * (root1 * root1), 0.0)
                f2 = jnp.where(row > j + 1, (c2 - c1 * ratio) * (root2 * root2), 0.0)
                s1, s2 = s[j : j + 1, :], s[j + 1 : j + 2, :]
                n1, n2 = n[j : j + 1, :], n[j + 1 : j + 2, :]
                packed[t] = s - f1 * s1 - f2 * (s2 - ratio * s1)
                inverse[t] = n - f1 * n1 - f2 * (n2 - ratio * n1)
        packed = [jnp.where(lane % block >= row, s * c, 0.0) for s, c in zip(packed, scales)]
        inverse = [n * c for n, c in zip(inverse, scales)]
        for e in range(experts):
            t, g = e // groups, e % groups
            work[e, lo:hi, lo:hi] = jnp.eye(block, dtype=jnp.float32)
            strip = exact_dot(
                inverse[t][:, g * block : (g + 1) * block], work[e, lo:hi, :], ((1,), (0,))
            )
            if lo:
                upper_ref[e, lo:hi, :lo] = jnp.zeros((block, lo), jnp.float32)
            upper_ref[e, lo:hi, lo:hi] = packed[t][:, g * block : (g + 1) * block]
            work[e, lo:hi, :] = strip
            if hi < size:
                upper_ref[e, lo:hi, hi:] = strip[:, hi:]
                work[e, hi:, lo:hi] = jnp.zeros((size - hi, block), jnp.float32)
                work[e, hi:, :] = work[e, hi:, :] - exact_dot(strip[:, hi:], strip, ((0,), (0,)))
    rows = lax.broadcasted_iota(jnp.int32, (size, size), 0)
    cols = lax.broadcasted_iota(jnp.int32, (size, size), 1)
    for e in range(experts):
        whole = jnp.where(rows >= cols, work[e], 0.0)
        high = whole.astype(jnp.bfloat16)
        inverse_ref[0, e] = high
        inverse_ref[1, e] = (whole - high.astype(jnp.float32)).astype(jnp.bfloat16)


def factorize(grams):
    experts, _, half, _ = grams.shape
    square = (experts, 2 * half, 2 * half)
    return pl.pallas_call(
        functools.partial(factor_kernel, block=BLOCK),
        in_specs=[WHOLE],
        out_specs=(WHOLE, WHOLE),
        out_shape=(
            jax.ShapeDtypeStruct(square, jnp.float32),
            jax.ShapeDtypeStruct((2,) + square, jnp.bfloat16),
        ),
        scratch_shapes=[pltpu.VMEM(square, jnp.float32)],
        compiler_params=params(24),
        name="factorize",
    )(grams)


def whiten_kernel(at_ref, mine_ref, other_ref, *refs, capacity):
    *row_refs, codes_ref = refs
    count = mine_ref.shape[1]
    y, x, core = at_ref[0], at_ref[1], at_ref[2]
    across = (((1,), (1,)), ((), ()))
    terms = [
        [
            jnp.where(core == e // count, mine_ref[term, e % count], other_ref[term, e % count])
            for term in range(2)
        ]
        for e in range(2 * count)
    ]
    for away, rows_ref in zip((0, 1, -1, 2), row_refs):
        found = [
            sum(
                lax.dot_general(rows_ref[e], term, across, preferred_element_type=jnp.float32)
                for term in terms[e]
            )
            for e in range(2 * count)
        ]
        for i, step in enumerate(NEAR):
            owner = lax.rem(y + step + SIDE, SIDE) * SIDE + lax.rem(x + away + SIDE, SIDE)
            own = slice(i * capacity, (i + 1) * capacity)
            codes_ref[owner] = jnp.concatenate([f[own] for f in found], axis=0).astype(
                codes_ref.dtype
            )


def whiten(at, mine, other, rows, capacity):
    _, count, size, _ = mine.shape
    return pl.pallas_call(
        functools.partial(whiten_kernel, capacity=capacity),
        in_specs=[SCALARS] + [WHOLE] * (2 + len(rows)),
        out_specs=WHOLE,
        out_shape=jax.ShapeDtypeStruct((SIDE * SIDE, 2 * count * capacity, size), jnp.bfloat16),
        compiler_params=params(24),
        name="whiten",
    )(at, mine, other, *rows)


def place_kernel(slot_ref, rows_ref, out_ref, *, width):
    tokens, top_k = slot_ref.shape
    count = tokens * top_k
    spread = jnp.broadcast_to(slot_ref[...][:, None, :], (tokens, top_k, top_k))
    lane = lax.broadcasted_iota(jnp.int32, (count, top_k), 1)
    row = lax.broadcasted_iota(jnp.int32, (count, top_k), 0)
    own = jnp.where(lane == row % top_k, spread.reshape(count, top_k), 0.0)
    slot = jnp.sum(own, axis=1, keepdims=True)
    column = lax.broadcasted_iota(jnp.int32, (count, width), 1).astype(jnp.float32)
    total = jnp.zeros(out_ref.shape, jnp.float32)
    for first in range(0, rows_ref.shape[0], width):
        pick = jnp.where(slot - float(first) == column, 1.0, 0.0).astype(rows_ref.dtype)
        total += dot(pick, rows_ref[first : first + width, :])
    out_ref[...] = total.astype(out_ref.dtype)


def place(slot, rows, step=128, width=512):
    tokens, top_k = slot.shape
    return pl.pallas_call(
        functools.partial(place_kernel, width=width),
        grid=(tokens // step,),
        in_specs=[
            pl.BlockSpec((step, top_k), lambda i: (i, 0)),
            pl.BlockSpec(rows.shape, lambda i: (0, 0)),
        ],
        out_specs=pl.BlockSpec((step * top_k, rows.shape[1]), lambda i: (i, 0)),
        out_shape=jax.ShapeDtypeStruct((tokens * top_k, rows.shape[1]), rows.dtype),
        compiler_params=params(40),
        name="place",
    )(slot, rows)


def slot_ranks(ids, first, experts):
    blocks, rows, _ = ids.shape
    wanted = first + jnp.arange(experts, dtype=jnp.int32)
    named = (jnp.swapaxes(ids, 1, 2)[:, :, None, :] == wanted[None, None, :, None]).any(axis=1)
    later = jnp.arange(rows)[:, None] < jnp.arange(rows)[None, :]
    rank = dot(named.reshape(-1, rows).astype(jnp.bfloat16), later.astype(jnp.bfloat16))
    return jnp.where(named, rank.reshape(named.shape), -1.0)


def sum_over_tok(mine, other):
    shape = mine.shape
    lanes = shape[-1]
    layers = lax.axis_size("z")
    mine = mine + shift(other, "c", 1)
    pieces = lax.all_to_all(mine.reshape(layers, -1, lanes), "z", 0, 0, tiled=True)
    return lax.all_gather(jnp.sum(pieces, axis=0), "z", tiled=True).reshape(shape)


def local(tokens, first_factor, expert_ids):
    groups = lax.axis_size(("y", "x"))
    tok_ranks = lax.axis_size(("z", "c"))
    per_group, model_dim, rank_k = first_factor.shape
    tok_rows, top_k = expert_ids.shape
    experts = groups * per_group
    capacity = tok_rows * top_k * 5 // (4 * experts)
    gram_scale = experts / (top_k * tok_rows * tok_ranks * groups)
    y, x, core = lax.axis_index("y"), lax.axis_index("x"), lax.axis_index("c")
    at = jnp.stack([y, x, core]).astype(jnp.int32)

    depth = model_dim // 2
    thin = depth // tok_ranks
    thick = depth // 2
    middle = per_group // 2
    half_rows = tok_rows // 2
    tied = lax.optimization_barrier
    lanes = 128
    tagged = jnp.concatenate(
        [tokens, jnp.pad(expert_ids.astype(tokens.dtype), ((0, 0), (0, lanes - top_k)))], axis=1
    )
    slices = lax.dynamic_slice_in_dim(first_factor, lax.axis_index(("z", "c")) * thin, thin, 1)
    thick_slice = lax.dynamic_slice_in_dim(first_factor, depth + core * thick, thick, 1)
    slices_before, slices_after, slices_far = shift(slices, "x", 1), shift(slices, "x", -1), shift(slices, "x", 2)
    tagged, thick_slice, slices_before, slices_after, slices_far = tied(
        (tagged, thick_slice, slices_before, slices_after, slices_far)
    )
    shared = lax.all_gather(jnp.stack([slices_before, slices_after, slices_far]), ("z", "c"))
    tokens_before, tokens_after, mine_before, mine_after = tied(
        (
            shift(tagged, "y", 1),
            shift(tagged, "y", -1),
            shift(thick_slice, "x", 1),
            shift(thick_slice, "x", -1),
        )
    )
    tokens_far = [shift(tokens_before[:half_rows], "y", 1), shift(tokens_after[half_rows:], "y", -1)]
    mine_far = [shift(mine_before[:middle], "x", 1), shift(mine_after[middle:], "x", -1)]
    ids_of = lambda a: a[:, model_dim : model_dim + top_k].astype(jnp.int32)
    first_of = y * SIDE * per_group
    near_ids = jnp.stack([expert_ids, ids_of(tokens_before)])
    near = select(
        slot_ranks(near_ids, first_of, SIDE * per_group),
        tokens,
        [tokens_before],
        capacity,
        model_dim,
    )
    near, mine_before, mine_after, *arrived = tied(
        (near, mine_before, mine_after, *tokens_far, *mine_far)
    )
    tokens_far, mine_far = arrived[:2], arrived[2:]
    far_ids = jnp.stack(
        [ids_of(tokens_after), jnp.concatenate([ids_of(a) for a in tokens_far], axis=0)]
    )
    far = select(
        slot_ranks(far_ids, first_of, SIDE * per_group),
        tokens_after,
        tokens_far,
        capacity,
        model_dim,
    )
    swap = lambda a: (a, shift(a, "c", 1))
    def projected(step, factors, start, count, index=None):
        where = jnp.stack([(x + step) % SIDE, core]).astype(jnp.int32)
        return project(where, near, far, factors, per_group, start, count, index)

    rows_own = projected(0, [first_factor], 0, per_group)
    near, far, rows_own, expert_ids = tied((near, far, rows_own, expert_ids))
    to_far = [
        projected(2, [shared, *swap(mine_far[i])], i * middle, middle, 2) for i in range(2)
    ]
    near, far, *to_far = tied((near, far, *to_far))
    from_after = shift(projected(-1, [shared, *swap(mine_before)], 0, per_group, 0), "x", -1)
    from_before = shift(projected(1, [shared, *swap(mine_after)], 0, per_group, 1), "x", 1)
    from_far = [shift(shift(a, "x", way), "x", way) for a, way in zip(to_far, (1, -1))]
    from_far = jnp.concatenate(from_far, axis=0)
    rows = [rows_own, from_after, from_before, from_far]

    upper, inverse = factorize(sum_over_tok(*partial_grams(at, rows, gram_scale)))
    codes = whiten(at, inverse, shift(inverse, "c", 1), rows, capacity)
    upper, codes = tied((upper, codes))
    returned = lax.all_to_all(codes, ("y", "x"), 0, 0, tiled=True)
    other = shift(upper, "c", 1)
    upper = jnp.where(
        core == 0, jnp.concatenate([upper, other]), jnp.concatenate([other, upper])
    )

    own_ranks = slot_ranks(expert_ids[None], 0, experts)[0]
    named = expert_ids.T[:, None, :] == jnp.arange(experts, dtype=jnp.int32)[None, :, None]
    slot = (expert_ids.T * capacity).astype(jnp.float32) + jnp.sum(
        jnp.where(named, own_ranks, 0.0), axis=1
    )
    gathered = place(slot.T, returned.reshape(experts * capacity, rank_k))
    return (gathered.reshape(tok_rows, top_k, rank_k), upper)


def solution(mesh):
    fine = Mesh(mesh.devices.reshape(-1, 2, SIDE, SIDE), ("z", "c", "y", "x"))
    every = ("z", "c", "y", "x")
    in_specs = (P(every, None), P(("y", "x"), None, None), P(every, None))
    out_specs = (P(every, None, None), P(("y", "x"), None, None))
    return jax.shard_map(local, mesh=fine, in_specs=in_specs, out_specs=out_specs, check_vma=False)
```

```python
import functools

import jax
import jax.numpy as jnp
from jax import lax
from jax.experimental import pallas as pl
from jax.experimental.pallas import tpu as pltpu
from jax.sharding import Mesh
from jax.sharding import PartitionSpec as P

RIDGE = 0.1
BLOCK = 32
SIDE = 4
NEAR = (0, -1, 1, 2)
WHOLE = pl.BlockSpec(memory_space=pltpu.VMEM)
SCALARS = pl.BlockSpec(memory_space=pltpu.SMEM)


def params(mebibytes):
    return pltpu.CompilerParams(vmem_limit_bytes=mebibytes * 2**20)


def exact_dot(a, b, dims):
    return lax.dot_general(
        a, b, (dims, ((), ())), precision=lax.Precision.HIGHEST, preferred_element_type=jnp.float32
    )


def dot(a, b):
    return jnp.dot(a, b, preferred_element_type=jnp.float32)


def shift(array, axis, step):
    size = lax.axis_size(axis)
    return lax.ppermute(array, axis, [(i, (i + step) % size) for i in range(size)])


def select_kernel(rank_ref, first_ref, *rest, capacity):
    *second_refs, out_ref, picks = rest
    experts, tok_rows = rank_ref.shape[1:]

    @pl.when(pl.program_id(0) == 0)
    def _():
        slots = lax.broadcasted_iota(jnp.int32, (capacity, tok_rows), 0).astype(jnp.float32)
        for source in range(2):
            for pair in range(experts // 2):
                both = [
                    jnp.where(rank_ref[source, e : e + 1, :] == slots, 1.0, 0.0)
                    for e in (2 * pair, 2 * pair + 1)
                ]
                picks[source, pair * 2 * capacity : (pair + 1) * 2 * capacity, :] = jnp.concatenate(
                    both, axis=0
                ).astype(jnp.bfloat16)

    blocks = (first_ref[...], jnp.concatenate([r[...] for r in second_refs], axis=0))
    step = 8
    for e in range(0, experts, step):
        rows = slice(e * capacity, (e + step) * capacity)
        found = [dot(picks[source, rows, :], blocks[source]) for source in range(2)]
        for i in range(step):
            own = slice(i * capacity, (i + 1) * capacity)
            out_ref[e + i] = jnp.concatenate([found[0][own], found[1][own]], axis=0).astype(
                out_ref.dtype
            )


def select(ranks, first, second, capacity, width, columns=512):
    _, experts, tok_rows = ranks.shape
    columns = min(columns, width)
    return pl.pallas_call(
        functools.partial(select_kernel, capacity=capacity),
        grid=(width // columns,),
        in_specs=[pl.BlockSpec(ranks.shape, lambda i: (0, 0, 0))]
        + [pl.BlockSpec((a.shape[0], columns), lambda i: (0, i)) for a in (first, *second)],
        out_specs=pl.BlockSpec((experts, 2 * capacity, columns), lambda i: (0, 0, i)),
        out_shape=jax.ShapeDtypeStruct((experts, 2 * capacity, width), first.dtype),
        scratch_shapes=[pltpu.VMEM((2, experts * capacity, tok_rows), jnp.bfloat16)],
        compiler_params=params(48),
        cost_estimate=pl.CostEstimate(
            flops=4 * experts * capacity * tok_rows * width, bytes_accessed=2**24, transcendentals=0
        ),
        name="select",
    )(ranks, first, *second)


def project_own_kernel(at_ref, near_ref, far_ref, factor_ref, out_ref):
    for i in range(out_ref.shape[0]):
        rows = jnp.concatenate([near_ref[i], far_ref[i]], axis=0)
        out_ref[i] = dot(rows, factor_ref[i]).astype(out_ref.dtype)


def project_kernel(at_ref, near_ref, far_ref, shared_ref, mine_ref, other_ref, out_ref):
    slices, _, _, thin, rank_k = shared_ref.shape
    half = mine_ref.shape[1]
    depth = slices * thin
    first = at_ref[1] == 0
    for i in range(out_ref.shape[0]):
        rows = jnp.concatenate([near_ref[i], far_ref[i]], axis=0)
        low, high = rows[:, depth : depth + half], rows[:, depth + half :]
        total = dot(rows[:, :depth], shared_ref[:, 0, i].reshape(depth, rank_k))
        total += dot(jnp.where(first, low, high), mine_ref[i])
        total += dot(jnp.where(first, high, low), other_ref[i])
        out_ref[i] = total.astype(out_ref.dtype)


def project(at, near, far, factors, per_group, start, count, index=None, step=2):
    width = near.shape[2]
    rank_k = factors[0].shape[-1]
    row_spec = lambda rows: pl.BlockSpec(
        (step, rows, width), lambda i, at: ((at[0] * per_group + start) // step + i, 0, 0)
    )
    plain = lambda a: pl.BlockSpec((step,) + a.shape[1:], lambda i, at: (i, 0, 0))
    if index is None:
        kernel, specs = project_own_kernel, [plain(factors[0])]
    else:
        shared = factors[0]
        kernel = project_kernel
        specs = [
            pl.BlockSpec(
                (shared.shape[0], 1, step) + shared.shape[3:],
                lambda i, at: (0, index, start // step + i, 0, 0),
            ),
            plain(factors[1]),
            plain(factors[2]),
        ]
    rows = near.shape[1] + far.shape[1]
    return pl.pallas_call(
        kernel,
        grid_spec=pltpu.PrefetchScalarGridSpec(
            num_scalar_prefetch=1,
            grid=(count // step,),
            in_specs=[row_spec(near.shape[1]), row_spec(far.shape[1])] + specs,
            out_specs=pl.BlockSpec((step, rows, rank_k), lambda i, at: (i, 0, 0)),
        ),
        out_shape=jax.ShapeDtypeStruct((count, rows, rank_k), near.dtype),
        compiler_params=params(48),
        cost_estimate=pl.CostEstimate(
            flops=2 * count * rows * width * rank_k,
            bytes_accessed=2 * count * width * (rows + rank_k),
            transcendentals=0,
        ),
        name="project",
    )(at, near, far, *factors)


def gram_kernel(at_ref, *refs, scale):
    *row_refs, mine_ref, other_ref = refs
    count, _, half, _ = mine_ref.shape
    core = at_ref[2]
    for out_ref, turn in ((mine_ref, core), (other_ref, 1 - core)):
        for i in range(count):
            rows = jnp.concatenate([r[turn * count + i] for r in row_refs], axis=0)
            lower, upper = rows[:, :half], rows[:, half:]
            transposed = ((0,), (0,))
            pairs = ((lower, lower), (lower, upper), (upper, upper))
            for block, (a, b) in enumerate(pairs):
                out_ref[i, block] = scale * lax.dot_general(
                    a, b, (transposed, ((), ())), preferred_element_type=jnp.float32
                )


def partial_grams(at, rows, scale):
    experts, _, rank_k = rows[0].shape
    half = jax.ShapeDtypeStruct((experts // 2, 3, rank_k // 2, rank_k // 2), jnp.float32)
    return pl.pallas_call(
        functools.partial(gram_kernel, scale=scale),
        in_specs=[SCALARS] + [WHOLE] * len(rows),
        out_specs=(WHOLE, WHOLE),
        out_shape=(half, half),
        compiler_params=params(16),
        name="grams",
    )(at, *rows)


def factor_kernel(gram_ref, upper_ref, inverse_ref, work, *, block):
    experts, _, half, _ = gram_ref.shape
    size = 2 * half
    lanes = 128
    groups = lanes // block
    tiles = experts // groups
    rows_h = lax.broadcasted_iota(jnp.int32, (half, half), 0)
    cols_h = lax.broadcasted_iota(jnp.int32, (half, half), 1)
    ridge_h = jnp.where(rows_h == cols_h, RIDGE, 0.0).astype(jnp.float32)
    for e in range(experts):
        work[e, :half, :half] = gram_ref[e, 0] + ridge_h
        work[e, :half, half:] = gram_ref[e, 1]
        work[e, half:, half:] = gram_ref[e, 2] + ridge_h
    lane = lax.broadcasted_iota(jnp.int32, (block, lanes), 1)
    row = lax.broadcasted_iota(jnp.int32, (block, lanes), 0)
    unit = jnp.where(lane % block == row, 1.0, 0.0).astype(jnp.float32)
    base = (lane // block) * block
    for k in range(size // block):
        lo, hi = k * block, (k + 1) * block
        packed = [
            jnp.concatenate([work[t * groups + g, lo:hi, lo:hi] for g in range(groups)], axis=1)
            for t in range(tiles)
        ]
        inverse = [unit for _ in range(tiles)]
        scales = [jnp.ones((block, lanes), jnp.float32) for _ in range(tiles)]
        for j in range(0, block, 2):
            for t in range(tiles):
                s, n = packed[t], inverse[t]
                c1 = jnp.take_along_axis(s, base + j, axis=1, mode="promise_in_bounds")
                c2 = jnp.take_along_axis(s, base + (j + 1), axis=1, mode="promise_in_bounds")
                beside = c1[j + 1 : j + 2, :]
                root1 = lax.rsqrt(c1[j : j + 1, :])
                ratio = beside * (root1 * root1)
                root2 = lax.rsqrt(c2[j + 1 : j + 2, :] - ratio * beside)
                scales[t] = jnp.where(row == j, root1, jnp.where(row == j + 1, root2, scales[t]))
                f1 = jnp.where(row > j, c1 * (root1 * root1), 0.0)
                f2 = jnp.where(row > j + 1, (c2 - c1 * ratio) * (root2 * root2), 0.0)
                s1, s2 = s[j : j + 1, :], s[j + 1 : j + 2, :]
                n1, n2 = n[j : j + 1, :], n[j + 1 : j + 2, :]
                packed[t] = s - f1 * s1 - f2 * (s2 - ratio * s1)
                inverse[t] = n - f1 * n1 - f2 * (n2 - ratio * n1)
        packed = [jnp.where(lane % block >= row, s * c, 0.0) for s, c in zip(packed, scales)]
        inverse = [n * c for n, c in zip(inverse, scales)]
        for e in range(experts):
            t, g = e // groups, e % groups
            work[e, lo:hi, lo:hi] = jnp.eye(block, dtype=jnp.float32)
            strip = exact_dot(
                inverse[t][:, g * block : (g + 1) * block], work[e, lo:hi, :], ((1,), (0,))
            )
            if lo:
                upper_ref[e, lo:hi, :lo] = jnp.zeros((block, lo), jnp.float32)
            upper_ref[e, lo:hi, lo:hi] = packed[t][:, g * block : (g + 1) * block]
            work[e, lo:hi, :] = strip
            if hi < size:
                upper_ref[e, lo:hi, hi:] = strip[:, hi:]
                work[e, hi:, lo:hi] = jnp.zeros((size - hi, block), jnp.float32)
                work[e, hi:, :] = work[e, hi:, :] - exact_dot(strip[:, hi:], strip, ((0,), (0,)))
    rows = lax.broadcasted_iota(jnp.int32, (size, size), 0)
    cols = lax.broadcasted_iota(jnp.int32, (size, size), 1)
    for e in range(experts):
        whole = jnp.where(rows >= cols, work[e], 0.0)
        high = whole.astype(jnp.bfloat16)
        inverse_ref[0, e] = high
        inverse_ref[1, e] = (whole - high.astype(jnp.float32)).astype(jnp.bfloat16)


def factorize(grams):
    experts, _, half, _ = grams.shape
    square = (experts, 2 * half, 2 * half)
    return pl.pallas_call(
        functools.partial(factor_kernel, block=BLOCK),
        in_specs=[WHOLE],
        out_specs=(WHOLE, WHOLE),
        out_shape=(
            jax.ShapeDtypeStruct(square, jnp.float32),
            jax.ShapeDtypeStruct((2,) + square, jnp.bfloat16),
        ),
        scratch_shapes=[pltpu.VMEM(square, jnp.float32)],
        compiler_params=params(24),
        name="factorize",
    )(grams)


def whiten_kernel(at_ref, mine_ref, other_ref, *refs, capacity):
    *row_refs, codes_ref = refs
    count = mine_ref.shape[1]
    y, x, core = at_ref[0], at_ref[1], at_ref[2]
    across = (((1,), (1,)), ((), ()))
    terms = [
        [
            jnp.where(core == e // count, mine_ref[term, e % count], other_ref[term, e % count])
            for term in range(2)
        ]
        for e in range(2 * count)
    ]
    for away, rows_ref in zip((0, 1, -1, 2), row_refs):
        found = [
            sum(
                lax.dot_general(rows_ref[e], term, across, preferred_element_type=jnp.float32)
                for term in terms[e]
            )
            for e in range(2 * count)
        ]
        for i, step in enumerate(NEAR):
            owner = lax.rem(y + step + SIDE, SIDE) * SIDE + lax.rem(x + away + SIDE, SIDE)
            own = slice(i * capacity, (i + 1) * capacity)
            codes_ref[owner] = jnp.concatenate([f[own] for f in found], axis=0).astype(
                codes_ref.dtype
            )


def whiten(at, mine, other, rows, capacity):
    _, count, size, _ = mine.shape
    return pl.pallas_call(
        functools.partial(whiten_kernel, capacity=capacity),
        in_specs=[SCALARS] + [WHOLE] * (2 + len(rows)),
        out_specs=WHOLE,
        out_shape=jax.ShapeDtypeStruct((SIDE * SIDE, 2 * count * capacity, size), jnp.bfloat16),
        compiler_params=params(24),
        name="whiten",
    )(at, mine, other, *rows)


def place_kernel(slot_ref, rows_ref, out_ref, *, width):
    tokens, top_k = slot_ref.shape
    count = tokens * top_k
    spread = jnp.broadcast_to(slot_ref[...][:, None, :], (tokens, top_k, top_k))
    lane = lax.broadcasted_iota(jnp.int32, (count, top_k), 1)
    row = lax.broadcasted_iota(jnp.int32, (count, top_k), 0)
    own = jnp.where(lane == row % top_k, spread.reshape(count, top_k), 0.0)
    slot = jnp.sum(own, axis=1, keepdims=True)
    column = lax.broadcasted_iota(jnp.int32, (count, width), 1).astype(jnp.float32)
    total = jnp.zeros(out_ref.shape, jnp.float32)
    for first in range(0, rows_ref.shape[0], width):
        pick = jnp.where(slot - float(first) == column, 1.0, 0.0).astype(rows_ref.dtype)
        total += dot(pick, rows_ref[first : first + width, :])
    out_ref[...] = total.astype(out_ref.dtype)


def place(slot, rows, step=128, width=512):
    tokens, top_k = slot.shape
    return pl.pallas_call(
        functools.partial(place_kernel, width=width),
        grid=(tokens // step,),
        in_specs=[
            pl.BlockSpec((step, top_k), lambda i: (i, 0)),
            pl.BlockSpec(rows.shape, lambda i: (0, 0)),
        ],
        out_specs=pl.BlockSpec((step * top_k, rows.shape[1]), lambda i: (i, 0)),
        out_shape=jax.ShapeDtypeStruct((tokens * top_k, rows.shape[1]), rows.dtype),
        compiler_params=params(40),
        name="place",
    )(slot, rows)


def slot_ranks(ids, first, experts):
    blocks, rows, _ = ids.shape
    wanted = first + jnp.arange(experts, dtype=jnp.int32)
    named = (jnp.swapaxes(ids, 1, 2)[:, :, None, :] == wanted[None, None, :, None]).any(axis=1)
    later = jnp.arange(rows)[:, None] < jnp.arange(rows)[None, :]
    rank = dot(named.reshape(-1, rows).astype(jnp.bfloat16), later.astype(jnp.bfloat16))
    return jnp.where(named, rank.reshape(named.shape), -1.0)


def sum_over_tok(mine, other):
    shape = mine.shape
    lanes = shape[-1]
    layers = lax.axis_size("z")
    mine = mine + shift(other, "c", 1)
    pieces = lax.all_to_all(mine.reshape(layers, -1, lanes), "z", 0, 0, tiled=True)
    return lax.all_gather(jnp.sum(pieces, axis=0), "z", tiled=True).reshape(shape)


def local(tokens, first_factor, expert_ids):
    groups = lax.axis_size(("y", "x"))
    tok_ranks = lax.axis_size(("z", "c"))
    per_group, model_dim, rank_k = first_factor.shape
    tok_rows, top_k = expert_ids.shape
    experts = groups * per_group
    capacity = tok_rows * top_k * 5 // (4 * experts)
    gram_scale = experts / (top_k * tok_rows * tok_ranks * groups)
    y, x, core = lax.axis_index("y"), lax.axis_index("x"), lax.axis_index("c")
    at = jnp.stack([y, x, core]).astype(jnp.int32)

    depth = model_dim // 2
    thin = depth // tok_ranks
    thick = depth // 2
    middle = per_group // 2
    half_rows = tok_rows // 2
    tied = lax.optimization_barrier
    lanes = 128
    tagged = jnp.concatenate(
        [tokens, jnp.pad(expert_ids.astype(tokens.dtype), ((0, 0), (0, lanes - top_k)))], axis=1
    )
    slices = lax.dynamic_slice_in_dim(first_factor, lax.axis_index(("z", "c")) * thin, thin, 1)
    thick_slice = lax.dynamic_slice_in_dim(first_factor, depth + core * thick, thick, 1)
    slices_before, slices_after, slices_far = shift(slices, "x", 1), shift(slices, "x", -1), shift(slices, "x", 2)
    tagged, thick_slice, slices_before, slices_after, slices_far = tied(
        (tagged, thick_slice, slices_before, slices_after, slices_far)
    )
    shared = lax.all_gather(jnp.stack([slices_before, slices_after, slices_far]), ("z", "c"))
    tokens_before, tokens_after, mine_before, mine_after = tied(
        (
            shift(tagged, "y", 1),
            shift(tagged, "y", -1),
            shift(thick_slice, "x", 1),
            shift(thick_slice, "x", -1),
        )
    )
    tokens_far = [shift(tokens_before[:half_rows], "y", 1), shift(tokens_after[half_rows:], "y", -1)]
    mine_far = [shift(mine_before[:middle], "x", 1), shift(mine_after[middle:], "x", -1)]
    ids_of = lambda a: a[:, model_dim : model_dim + top_k].astype(jnp.int32)
    first_of = y * SIDE * per_group
    near_ids = jnp.stack([expert_ids, ids_of(tokens_before)])
    near = select(
        slot_ranks(near_ids, first_of, SIDE * per_group),
        tokens,
        [tokens_before],
        capacity,
        model_dim,
    )
    near, *tokens_far = tied((near, *tokens_far))
    far_ids = jnp.stack(
        [ids_of(tokens_after), jnp.concatenate([ids_of(a) for a in tokens_far], axis=0)]
    )
    far = select(
        slot_ranks(far_ids, first_of, SIDE * per_group),
        tokens_after,
        tokens_far,
        capacity,
        model_dim,
    )
    far, mine_before, mine_after, *mine_far = tied((far, mine_before, mine_after, *mine_far))
    other_far = [shift(a, "c", 1) for a in mine_far]
    mine_before, mine_after, *other_far = tied((mine_before, mine_after, *other_far))
    other_before, other_after = shift(mine_before, "c", 1), shift(mine_after, "c", 1)

    def projected(step, factors, start, count, index=None):
        where = jnp.stack([(x + step) % SIDE, core]).astype(jnp.int32)
        return project(where, near, far, factors, per_group, start, count, index)

    to_far = [
        projected(2, [shared, mine_far[i], other_far[i]], i * middle, middle, 2) for i in range(2)
    ]
    near, far, *to_far = tied((near, far, *to_far))
    from_far = [shift(shift(a, "x", way), "x", way) for a, way in zip(to_far, (1, -1))]
    to_before = projected(-1, [shared, mine_before, other_before], 0, per_group, 0)
    near, far, to_before = tied((near, far, to_before))
    from_after = shift(to_before, "x", -1)
    to_after = projected(1, [shared, mine_after, other_after], 0, per_group, 1)
    near, far, to_after = tied((near, far, to_after))
    from_before = shift(to_after, "x", 1)
    rows_own = projected(0, [first_factor], 0, per_group)
    rows_own, expert_ids = tied((rows_own, expert_ids))
    from_far = jnp.concatenate(from_far, axis=0)
    rows = [rows_own, from_after, from_before, from_far]

    upper, inverse = factorize(sum_over_tok(*partial_grams(at, rows, gram_scale)))
    codes = whiten(at, inverse, shift(inverse, "c", 1), rows, capacity)
    upper, codes = tied((upper, codes))
    returned = lax.all_to_all(codes, ("y", "x"), 0, 0, tiled=True)
    other = shift(upper, "c", 1)
    upper = jnp.where(
        core == 0, jnp.concatenate([upper, other]), jnp.concatenate([other, upper])
    )

    own_ranks = slot_ranks(expert_ids[None], 0, experts)[0]
    named = expert_ids.T[:, None, :] == jnp.arange(experts, dtype=jnp.int32)[None, :, None]
    slot = (expert_ids.T * capacity).astype(jnp.float32) + jnp.sum(
        jnp.where(named, own_ranks, 0.0), axis=1
    )
    gathered = place(slot.T, returned.reshape(experts * capacity, rank_k))
    return (gathered.reshape(tok_rows, top_k, rank_k), upper)


def solution(mesh):
    fine = Mesh(mesh.devices.reshape(-1, 2, SIDE, SIDE), ("z", "c", "y", "x"))
    every = ("z", "c", "y", "x")
    in_specs = (P(every, None), P(("y", "x"), None, None), P(every, None))
    out_specs = (P(every, None, None), P(("y", "x"), None, None))
    return jax.shard_map(local, mesh=fine, in_specs=in_specs, out_specs=out_specs, check_vma=False)
```

```python
import functools

import jax
import jax.numpy as jnp
from jax import lax
from jax.experimental import pallas as pl
from jax.experimental.pallas import tpu as pltpu
from jax.sharding import Mesh
from jax.sharding import PartitionSpec as P

RIDGE = 0.1
BLOCK = 64
SIDE = 4
NEAR = (0, -1, 1, 2)
WHOLE = pl.BlockSpec(memory_space=pltpu.VMEM)
SCALARS = pl.BlockSpec(memory_space=pltpu.SMEM)


def params(mebibytes):
    return pltpu.CompilerParams(vmem_limit_bytes=mebibytes * 2**20)


def exact_dot(a, b, dims):
    return lax.dot_general(
        a, b, (dims, ((), ())), precision=lax.Precision.HIGHEST, preferred_element_type=jnp.float32
    )


def dot(a, b):
    return jnp.dot(a, b, preferred_element_type=jnp.float32)


def shift(array, axis, step):
    size = lax.axis_size(axis)
    return lax.ppermute(array, axis, [(i, (i + step) % size) for i in range(size)])


def select_kernel(rank_ref, first_ref, *rest, capacity):
    *second_refs, out_ref, picks = rest
    experts, tok_rows = rank_ref.shape[1:]

    @pl.when(pl.program_id(0) == 0)
    def _():
        slots = lax.broadcasted_iota(jnp.int32, (capacity, tok_rows), 0).astype(jnp.float32)
        for source in range(2):
            for pair in range(experts // 2):
                both = [
                    jnp.where(rank_ref[source, e : e + 1, :] == slots, 1.0, 0.0)
                    for e in (2 * pair, 2 * pair + 1)
                ]
                picks[source, pair * 2 * capacity : (pair + 1) * 2 * capacity, :] = jnp.concatenate(
                    both, axis=0
                ).astype(jnp.bfloat16)

    blocks = (first_ref[...], jnp.concatenate([r[...] for r in second_refs], axis=0))
    step = 8
    for e in range(0, experts, step):
        rows = slice(e * capacity, (e + step) * capacity)
        found = [dot(picks[source, rows, :], blocks[source]) for source in range(2)]
        for i in range(step):
            own = slice(i * capacity, (i + 1) * capacity)
            out_ref[e + i] = jnp.concatenate([found[0][own], found[1][own]], axis=0).astype(
                out_ref.dtype
            )


def select(ranks, first, second, capacity, width, columns=512):
    _, experts, tok_rows = ranks.shape
    columns = min(columns, width)
    return pl.pallas_call(
        functools.partial(select_kernel, capacity=capacity),
        grid=(width // columns,),
        in_specs=[pl.BlockSpec(ranks.shape, lambda i: (0, 0, 0))]
        + [pl.BlockSpec((a.shape[0], columns), lambda i: (0, i)) for a in (first, *second)],
        out_specs=pl.BlockSpec((experts, 2 * capacity, columns), lambda i: (0, 0, i)),
        out_shape=jax.ShapeDtypeStruct((experts, 2 * capacity, width), first.dtype),
        scratch_shapes=[pltpu.VMEM((2, experts * capacity, tok_rows), jnp.bfloat16)],
        compiler_params=params(48),
        cost_estimate=pl.CostEstimate(
            flops=4 * experts * capacity * tok_rows * width, bytes_accessed=2**24, transcendentals=0
        ),
        name="select",
    )(ranks, first, *second)


def project_own_kernel(at_ref, near_ref, far_ref, factor_ref, out_ref):
    for i in range(out_ref.shape[0]):
        rows = jnp.concatenate([near_ref[i], far_ref[i]], axis=0)
        out_ref[i] = dot(rows, factor_ref[i]).astype(out_ref.dtype)


def project_kernel(at_ref, near_ref, far_ref, shared_ref, mine_ref, other_ref, out_ref):
    slices, _, _, thin, rank_k = shared_ref.shape
    half = mine_ref.shape[1]
    depth = slices * thin
    first = at_ref[1] == 0
    for i in range(out_ref.shape[0]):
        rows = jnp.concatenate([near_ref[i], far_ref[i]], axis=0)
        low, high = rows[:, depth : depth + half], rows[:, depth + half :]
        total = dot(rows[:, :depth], shared_ref[:, 0, i].reshape(depth, rank_k))
        total += dot(jnp.where(first, low, high), mine_ref[i])
        total += dot(jnp.where(first, high, low), other_ref[i])
        out_ref[i] = total.astype(out_ref.dtype)


def project(at, near, far, factors, per_group, start, count, index=None, step=2):
    width = near.shape[2]
    rank_k = factors[0].shape[-1]
    row_spec = lambda rows: pl.BlockSpec(
        (step, rows, width), lambda i, at: ((at[0] * per_group + start) // step + i, 0, 0)
    )
    plain = lambda a: pl.BlockSpec((step,) + a.shape[1:], lambda i, at: (i, 0, 0))
    if index is None:
        kernel, specs = project_own_kernel, [plain(factors[0])]
    else:
        shared = factors[0]
        kernel = project_kernel
        specs = [
            pl.BlockSpec(
                (shared.shape[0], 1, step) + shared.shape[3:],
                lambda i, at: (0, index, start // step + i, 0, 0),
            ),
            plain(factors[1]),
            plain(factors[2]),
        ]
    rows = near.shape[1] + far.shape[1]
    return pl.pallas_call(
        kernel,
        grid_spec=pltpu.PrefetchScalarGridSpec(
            num_scalar_prefetch=1,
            grid=(count // step,),
            in_specs=[row_spec(near.shape[1]), row_spec(far.shape[1])] + specs,
            out_specs=pl.BlockSpec((step, rows, rank_k), lambda i, at: (i, 0, 0)),
        ),
        out_shape=jax.ShapeDtypeStruct((count, rows, rank_k), near.dtype),
        compiler_params=params(48),
        cost_estimate=pl.CostEstimate(
            flops=2 * count * rows * width * rank_k,
            bytes_accessed=2 * count * width * (rows + rank_k),
            transcendentals=0,
        ),
        name="project",
    )(at, near, far, *factors)


def gram_kernel(at_ref, *refs, scale):
    *row_refs, mine_ref, other_ref = refs
    count, _, half, _ = mine_ref.shape
    core = at_ref[2]
    for out_ref, turn in ((mine_ref, core), (other_ref, 1 - core)):
        for i in range(count):
            rows = jnp.concatenate([r[turn * count + i] for r in row_refs], axis=0)
            lower, upper = rows[:, :half], rows[:, half:]
            transposed = ((0,), (0,))
            pairs = ((lower, lower), (lower, upper), (upper, upper))
            for block, (a, b) in enumerate(pairs):
                out_ref[i, block] = scale * lax.dot_general(
                    a, b, (transposed, ((), ())), preferred_element_type=jnp.float32
                )


def partial_grams(at, rows, scale):
    experts, _, rank_k = rows[0].shape
    half = jax.ShapeDtypeStruct((experts // 2, 3, rank_k // 2, rank_k // 2), jnp.float32)
    return pl.pallas_call(
        functools.partial(gram_kernel, scale=scale),
        in_specs=[SCALARS] + [WHOLE] * len(rows),
        out_specs=(WHOLE, WHOLE),
        out_shape=(half, half),
        compiler_params=params(16),
        name="grams",
    )(at, *rows)


def factor_kernel(gram_ref, upper_ref, inverse_ref, work, *, block):
    experts, _, half, _ = gram_ref.shape
    size = 2 * half
    lanes = 128
    groups = lanes // block
    tiles = experts // groups
    rows_h = lax.broadcasted_iota(jnp.int32, (half, half), 0)
    cols_h = lax.broadcasted_iota(jnp.int32, (half, half), 1)
    ridge_h = jnp.where(rows_h == cols_h, RIDGE, 0.0).astype(jnp.float32)
    for e in range(experts):
        work[e, :half, :half] = gram_ref[e, 0] + ridge_h
        work[e, :half, half:] = gram_ref[e, 1]
        work[e, half:, half:] = gram_ref[e, 2] + ridge_h
    lane = lax.broadcasted_iota(jnp.int32, (block, lanes), 1)
    row = lax.broadcasted_iota(jnp.int32, (block, lanes), 0)
    unit = jnp.where(lane % block == row, 1.0, 0.0).astype(jnp.float32)
    base = (lane // block) * block
    for k in range(size // block):
        lo, hi = k * block, (k + 1) * block
        packed = [
            jnp.concatenate([work[t * groups + g, lo:hi, lo:hi] for g in range(groups)], axis=1)
            for t in range(tiles)
        ]
        inverse = [unit for _ in range(tiles)]
        scales = [jnp.ones((block, lanes), jnp.float32) for _ in range(tiles)]
        for j in range(0, block, 4):
            for t in range(tiles):
                s, n = packed[t], inverse[t]
                columns = [
                    jnp.take_along_axis(s, base + (j + i), axis=1, mode="promise_in_bounds")
                    for i in range(4)
                ]
                heads = [s[j + i : j + i + 1, :] for i in range(4)]
                tails = [n[j + i : j + i + 1, :] for i in range(4)]
                for i in range(4):
                    at = j + i
                    root = lax.rsqrt(columns[i][at : at + 1, :])
                    inv = root * root
                    scales[t] = jnp.where(row == at, root, scales[t])
                    factor = jnp.where(row > at, columns[i] * inv, 0.0)
                    for m in range(i + 1, 4):
                        ratio = columns[m][at : at + 1, :] * inv
                        columns[m] = columns[m] - columns[i] * ratio
                    s = s - factor * heads[i]
                    n = n - factor * tails[i]
                    for m in range(i + 1, 4):
                        ratio = factor[j + m : j + m + 1, :]
                        heads[m] = heads[m] - ratio * heads[i]
                        tails[m] = tails[m] - ratio * tails[i]
                packed[t], inverse[t] = s, n
        packed = [jnp.where(lane % block >= row, s * c, 0.0) for s, c in zip(packed, scales)]
        inverse = [n * c for n, c in zip(inverse, scales)]
        for e in range(experts):
            t, g = e // groups, e % groups
            work[e, lo:hi, lo:hi] = jnp.eye(block, dtype=jnp.float32)
            strip = exact_dot(
                inverse[t][:, g * block : (g + 1) * block], work[e, lo:hi, :], ((1,), (0,))
            )
            if lo:
                upper_ref[e, lo:hi, :lo] = jnp.zeros((block, lo), jnp.float32)
            upper_ref[e, lo:hi, lo:hi] = packed[t][:, g * block : (g + 1) * block]
            work[e, lo:hi, :] = strip
            if hi < size:
                upper_ref[e, lo:hi, hi:] = strip[:, hi:]
                work[e, hi:, lo:hi] = jnp.zeros((size - hi, block), jnp.float32)
                work[e, hi:, :] = work[e, hi:, :] - exact_dot(strip[:, hi:], strip, ((0,), (0,)))
    rows = lax.broadcasted_iota(jnp.int32, (size, size), 0)
    cols = lax.broadcasted_iota(jnp.int32, (size, size), 1)
    for e in range(experts):
        whole = jnp.where(rows >= cols, work[e], 0.0)
        high = whole.astype(jnp.bfloat16)
        inverse_ref[0, e] = high
        inverse_ref[1, e] = (whole - high.astype(jnp.float32)).astype(jnp.bfloat16)


def factorize(grams):
    experts, _, half, _ = grams.shape
    square = (experts, 2 * half, 2 * half)
    return pl.pallas_call(
        functools.partial(factor_kernel, block=BLOCK),
        in_specs=[WHOLE],
        out_specs=(WHOLE, WHOLE),
        out_shape=(
            jax.ShapeDtypeStruct(square, jnp.float32),
            jax.ShapeDtypeStruct((2,) + square, jnp.bfloat16),
        ),
        scratch_shapes=[pltpu.VMEM(square, jnp.float32)],
        compiler_params=params(24),
        name="factorize",
    )(grams)


def whiten_kernel(at_ref, mine_ref, other_ref, *refs, capacity):
    *row_refs, codes_ref = refs
    count = mine_ref.shape[1]
    y, x, core = at_ref[0], at_ref[1], at_ref[2]
    across = (((1,), (1,)), ((), ()))
    terms = [
        [
            jnp.where(core == e // count, mine_ref[term, e % count], other_ref[term, e % count])
            for term in range(2)
        ]
        for e in range(2 * count)
    ]
    for away, rows_ref in zip((0, 1, -1, 2), row_refs):
        found = [
            sum(
                lax.dot_general(rows_ref[e], term, across, preferred_element_type=jnp.float32)
                for term in terms[e]
            )
            for e in range(2 * count)
        ]
        for i, step in enumerate(NEAR):
            owner = lax.rem(y + step + SIDE, SIDE) * SIDE + lax.rem(x + away + SIDE, SIDE)
            own = slice(i * capacity, (i + 1) * capacity)
            codes_ref[owner] = jnp.concatenate([f[own] for f in found], axis=0).astype(
                codes_ref.dtype
            )


def whiten(at, mine, other, rows, capacity):
    _, count, size, _ = mine.shape
    return pl.pallas_call(
        functools.partial(whiten_kernel, capacity=capacity),
        in_specs=[SCALARS] + [WHOLE] * (2 + len(rows)),
        out_specs=WHOLE,
        out_shape=jax.ShapeDtypeStruct((SIDE * SIDE, 2 * count * capacity, size), jnp.bfloat16),
        compiler_params=params(56),
        name="whiten",
    )(at, mine, other, *rows)


def place_kernel(slot_ref, rows_ref, out_ref, *, width):
    tokens, top_k = slot_ref.shape
    count = tokens * top_k
    spread = jnp.broadcast_to(slot_ref[...][:, None, :], (tokens, top_k, top_k))
    lane = lax.broadcasted_iota(jnp.int32, (count, top_k), 1)
    row = lax.broadcasted_iota(jnp.int32, (count, top_k), 0)
    own = jnp.where(lane == row % top_k, spread.reshape(count, top_k), 0.0)
    slot = jnp.sum(own, axis=1, keepdims=True)
    column = lax.broadcasted_iota(jnp.int32, (count, width), 1).astype(jnp.float32)
    total = jnp.zeros(out_ref.shape, jnp.float32)
    for first in range(0, rows_ref.shape[0], width):
        pick = jnp.where(slot - float(first) == column, 1.0, 0.0).astype(rows_ref.dtype)
        total += dot(pick, rows_ref[first : first + width, :])
    out_ref[...] = total.astype(out_ref.dtype)


def place(slot, rows, step=128, width=512):
    tokens, top_k = slot.shape
    return pl.pallas_call(
        functools.partial(place_kernel, width=width),
        grid=(tokens // step,),
        in_specs=[
            pl.BlockSpec((step, top_k), lambda i: (i, 0)),
            pl.BlockSpec(rows.shape, lambda i: (0, 0)),
        ],
        out_specs=pl.BlockSpec((step * top_k, rows.shape[1]), lambda i: (i, 0)),
        out_shape=jax.ShapeDtypeStruct((tokens * top_k, rows.shape[1]), rows.dtype),
        compiler_params=params(40),
        name="place",
    )(slot, rows)


def slot_ranks(ids, first, experts):
    blocks, rows, _ = ids.shape
    wanted = first + jnp.arange(experts, dtype=jnp.int32)
    named = (jnp.swapaxes(ids, 1, 2)[:, :, None, :] == wanted[None, None, :, None]).any(axis=1)
    later = jnp.arange(rows)[:, None] < jnp.arange(rows)[None, :]
    rank = dot(named.reshape(-1, rows).astype(jnp.bfloat16), later.astype(jnp.bfloat16))
    return jnp.where(named, rank.reshape(named.shape), -1.0)


def sum_over_tok(mine, other):
    shape = mine.shape
    lanes = shape[-1]
    layers = lax.axis_size("z")
    mine = mine + shift(other, "c", 1)
    pieces = lax.all_to_all(mine.reshape(layers, -1, lanes), "z", 0, 0, tiled=True)
    return lax.all_gather(jnp.sum(pieces, axis=0), "z", tiled=True).reshape(shape)


def local(tokens, first_factor, expert_ids):
    groups = lax.axis_size(("y", "x"))
    tok_ranks = lax.axis_size(("z", "c"))
    per_group, model_dim, rank_k = first_factor.shape
    tok_rows, top_k = expert_ids.shape
    experts = groups * per_group
    capacity = tok_rows * top_k * 5 // (4 * experts)
    gram_scale = experts / (top_k * tok_rows * tok_ranks * groups)
    y, x, core = lax.axis_index("y"), lax.axis_index("x"), lax.axis_index("c")
    at = jnp.stack([y, x, core]).astype(jnp.int32)

    depth = model_dim // 2
    thin = depth // tok_ranks
    thick = depth // 2
    middle = per_group // 2
    half_rows = tok_rows // 2
    tied = lax.optimization_barrier
    lanes = 128
    tagged = jnp.concatenate(
        [tokens, jnp.pad(expert_ids.astype(tokens.dtype), ((0, 0), (0, lanes - top_k)))], axis=1
    )
    slices = lax.dynamic_slice_in_dim(first_factor, lax.axis_index(("z", "c")) * thin, thin, 1)
    thick_slice = lax.dynamic_slice_in_dim(first_factor, depth + core * thick, thick, 1)
    slices_before, slices_after, slices_far = shift(slices, "x", 1), shift(slices, "x", -1), shift(slices, "x", 2)
    tagged, thick_slice, slices_before, slices_after, slices_far = tied(
        (tagged, thick_slice, slices_before, slices_after, slices_far)
    )
    shared = lax.all_gather(jnp.stack([slices_before, slices_after, slices_far]), ("z", "c"))
    tokens_before, tokens_after, mine_before, mine_after = tied(
        (
            shift(tagged, "y", 1),
            shift(tagged, "y", -1),
            shift(thick_slice, "x", 1),
            shift(thick_slice, "x", -1),
        )
    )
    tokens_far = [shift(tokens_before[:half_rows], "y", 1), shift(tokens_after[half_rows:], "y", -1)]
    mine_far = [shift(mine_before[:middle], "x", 1), shift(mine_after[middle:], "x", -1)]
    ids_of = lambda a: a[:, model_dim : model_dim + top_k].astype(jnp.int32)
    first_of = y * SIDE * per_group
    near_ids = jnp.stack([expert_ids, ids_of(tokens_before)])
    near = select(
        slot_ranks(near_ids, first_of, SIDE * per_group),
        tokens,
        [tokens_before],
        capacity,
        model_dim,
    )
    near, *tokens_far = tied((near, *tokens_far))
    far_ids = jnp.stack(
        [ids_of(tokens_after), jnp.concatenate([ids_of(a) for a in tokens_far], axis=0)]
    )
    far = select(
        slot_ranks(far_ids, first_of, SIDE * per_group),
        tokens_after,
        tokens_far,
        capacity,
        model_dim,
    )
    far, mine_before, mine_after, *mine_far = tied((far, mine_before, mine_after, *mine_far))
    other_far = [shift(a, "c", 1) for a in mine_far]
    mine_before, mine_after, *other_far = tied((mine_before, mine_after, *other_far))
    other_before, other_after = shift(mine_before, "c", 1), shift(mine_after, "c", 1)

    def projected(step, factors, start, count, index=None):
        where = jnp.stack([(x + step) % SIDE, core]).astype(jnp.int32)
        return project(where, near, far, factors, per_group, start, count, index)

    to_far = [
        projected(2, [shared, mine_far[i], other_far[i]], i * middle, middle, 2) for i in range(2)
    ]
    near, far, *to_far = tied((near, far, *to_far))
    from_far = [shift(shift(a, "x", way), "x", way) for a, way in zip(to_far, (1, -1))]
    to_before = projected(-1, [shared, mine_before, other_before], 0, per_group, 0)
    near, far, to_before = tied((near, far, to_before))
    from_after = shift(to_before, "x", -1)
    to_after = projected(1, [shared, mine_after, other_after], 0, per_group, 1)
    near, far, to_after = tied((near, far, to_after))
    from_before = shift(to_after, "x", 1)
    rows_own = projected(0, [first_factor], 0, per_group)
    rows_own, expert_ids = tied((rows_own, expert_ids))
    from_far = jnp.concatenate(from_far, axis=0)
    rows = [rows_own, from_after, from_before, from_far]

    upper, inverse = factorize(sum_over_tok(*partial_grams(at, rows, gram_scale)))
    codes = whiten(at, inverse, shift(inverse, "c", 1), rows, capacity)
    upper, codes = tied((upper, codes))
    returned = lax.all_to_all(codes, ("y", "x"), 0, 0, tiled=True)
    other = shift(upper, "c", 1)
    upper = jnp.where(
        core == 0, jnp.concatenate([upper, other]), jnp.concatenate([other, upper])
    )

    own_ranks = slot_ranks(expert_ids[None], 0, experts)[0]
    named = expert_ids.T[:, None, :] == jnp.arange(experts, dtype=jnp.int32)[None, :, None]
    slot = (expert_ids.T * capacity).astype(jnp.float32) + jnp.sum(
        jnp.where(named, own_ranks, 0.0), axis=1
    )
    gathered = place(slot.T, returned.reshape(experts * capacity, rank_k))
    return (gathered.reshape(tok_rows, top_k, rank_k), upper)


def solution(mesh):
    fine = Mesh(mesh.devices.reshape(-1, 2, SIDE, SIDE), ("z", "c", "y", "x"))
    every = ("z", "c", "y", "x")
    in_specs = (P(every, None), P(("y", "x"), None, None), P(every, None))
    out_specs = (P(every, None, None), P(("y", "x"), None, None))
    return jax.shard_map(local, mesh=fine, in_specs=in_specs, out_specs=out_specs, check_vma=False)
```

```python
import functools

import jax
import jax.numpy as jnp
from jax import lax
from jax.experimental import pallas as pl
from jax.experimental.pallas import tpu as pltpu
from jax.sharding import Mesh
from jax.sharding import PartitionSpec as P

RIDGE = 0.1
BLOCK = 64
SIDE = 4
NEAR = (0, -1, 1, 2)
WHOLE = pl.BlockSpec(memory_space=pltpu.VMEM)
SCALARS = pl.BlockSpec(memory_space=pltpu.SMEM)


def params(mebibytes):
    return pltpu.CompilerParams(vmem_limit_bytes=mebibytes * 2**20)


def exact_dot(a, b, dims):
    return lax.dot_general(
        a, b, (dims, ((), ())), precision=lax.Precision.HIGHEST, preferred_element_type=jnp.float32
    )


def dot(a, b):
    return jnp.dot(a, b, preferred_element_type=jnp.float32)


def shift(array, axis, step):
    size = lax.axis_size(axis)
    return lax.ppermute(array, axis, [(i, (i + step) % size) for i in range(size)])


def select_kernel(rank_ref, first_ref, *rest, capacity):
    *second_refs, out_ref, picks = rest
    experts, tok_rows = rank_ref.shape[1:]

    @pl.when(pl.program_id(0) == 0)
    def _():
        slots = lax.broadcasted_iota(jnp.int32, (capacity, tok_rows), 0).astype(jnp.float32)
        for source in range(2):
            for pair in range(experts // 2):
                both = [
                    jnp.where(rank_ref[source, e : e + 1, :] == slots, 1.0, 0.0)
                    for e in (2 * pair, 2 * pair + 1)
                ]
                picks[source, pair * 2 * capacity : (pair + 1) * 2 * capacity, :] = jnp.concatenate(
                    both, axis=0
                ).astype(jnp.bfloat16)

    blocks = (first_ref[...], jnp.concatenate([r[...] for r in second_refs], axis=0))
    step = 8
    for e in range(0, experts, step):
        rows = slice(e * capacity, (e + step) * capacity)
        found = [dot(picks[source, rows, :], blocks[source]) for source in range(2)]
        for i in range(step):
            own = slice(i * capacity, (i + 1) * capacity)
            out_ref[e + i] = jnp.concatenate([found[0][own], found[1][own]], axis=0).astype(
                out_ref.dtype
            )


def select(ranks, first, second, capacity, width, columns=512):
    _, experts, tok_rows = ranks.shape
    columns = min(columns, width)
    return pl.pallas_call(
        functools.partial(select_kernel, capacity=capacity),
        grid=(width // columns,),
        in_specs=[pl.BlockSpec(ranks.shape, lambda i: (0, 0, 0))]
        + [pl.BlockSpec((a.shape[0], columns), lambda i: (0, i)) for a in (first, *second)],
        out_specs=pl.BlockSpec((experts, 2 * capacity, columns), lambda i: (0, 0, i)),
        out_shape=jax.ShapeDtypeStruct((experts, 2 * capacity, width), first.dtype),
        scratch_shapes=[pltpu.VMEM((2, experts * capacity, tok_rows), jnp.bfloat16)],
        compiler_params=params(48),
        cost_estimate=pl.CostEstimate(
            flops=4 * experts * capacity * tok_rows * width, bytes_accessed=2**24, transcendentals=0
        ),
        name="select",
    )(ranks, first, *second)


def project_own_kernel(at_ref, near_ref, far_ref, factor_ref, out_ref):
    for i in range(out_ref.shape[0]):
        rows = jnp.concatenate([near_ref[i], far_ref[i]], axis=0)
        out_ref[i] = dot(rows, factor_ref[i]).astype(out_ref.dtype)


def project_kernel(at_ref, near_ref, far_ref, shared_ref, mine_ref, other_ref, out_ref):
    slices, _, _, thin, rank_k = shared_ref.shape
    half = mine_ref.shape[1]
    depth = slices * thin
    first = at_ref[1] == 0
    for i in range(out_ref.shape[0]):
        rows = jnp.concatenate([near_ref[i], far_ref[i]], axis=0)
        low, high = rows[:, depth : depth + half], rows[:, depth + half :]
        total = dot(rows[:, :depth], shared_ref[:, 0, i].reshape(depth, rank_k))
        total += dot(jnp.where(first, low, high), mine_ref[i])
        total += dot(jnp.where(first, high, low), other_ref[i])
        out_ref[i] = total.astype(out_ref.dtype)


def project(at, near, far, factors, per_group, start, count, index=None, step=2):
    width = near.shape[2]
    rank_k = factors[0].shape[-1]
    row_spec = lambda rows: pl.BlockSpec(
        (step, rows, width), lambda i, at: ((at[0] * per_group + start) // step + i, 0, 0)
    )
    plain = lambda a: pl.BlockSpec((step,) + a.shape[1:], lambda i, at: (i, 0, 0))
    if index is None:
        kernel, specs = project_own_kernel, [plain(factors[0])]
    else:
        shared = factors[0]
        kernel = project_kernel
        specs = [
            pl.BlockSpec(
                (shared.shape[0], 1, step) + shared.shape[3:],
                lambda i, at: (0, index, start // step + i, 0, 0),
            ),
            plain(factors[1]),
            plain(factors[2]),
        ]
    rows = near.shape[1] + far.shape[1]
    return pl.pallas_call(
        kernel,
        grid_spec=pltpu.PrefetchScalarGridSpec(
            num_scalar_prefetch=1,
            grid=(count // step,),
            in_specs=[row_spec(near.shape[1]), row_spec(far.shape[1])] + specs,
            out_specs=pl.BlockSpec((step, rows, rank_k), lambda i, at: (i, 0, 0)),
        ),
        out_shape=jax.ShapeDtypeStruct((count, rows, rank_k), near.dtype),
        compiler_params=params(48),
        cost_estimate=pl.CostEstimate(
            flops=2 * count * rows * width * rank_k,
            bytes_accessed=2 * count * width * (rows + rank_k),
            transcendentals=0,
        ),
        name="project",
    )(at, near, far, *factors)


def gram_kernel(at_ref, *refs, scale):
    *row_refs, mine_ref, other_ref = refs
    count, _, half, _ = mine_ref.shape
    core = at_ref[2]
    for out_ref, turn in ((mine_ref, core), (other_ref, 1 - core)):
        for i in range(count):
            rows = jnp.concatenate([r[turn * count + i] for r in row_refs], axis=0)
            lower, upper = rows[:, :half], rows[:, half:]
            transposed = ((0,), (0,))
            pairs = ((lower, lower), (lower, upper), (upper, upper))
            for block, (a, b) in enumerate(pairs):
                out_ref[i, block] = scale * lax.dot_general(
                    a, b, (transposed, ((), ())), preferred_element_type=jnp.float32
                )


def partial_grams(at, rows, scale):
    experts, _, rank_k = rows[0].shape
    half = jax.ShapeDtypeStruct((experts // 2, 3, rank_k // 2, rank_k // 2), jnp.float32)
    return pl.pallas_call(
        functools.partial(gram_kernel, scale=scale),
        in_specs=[SCALARS] + [WHOLE] * len(rows),
        out_specs=(WHOLE, WHOLE),
        out_shape=(half, half),
        compiler_params=params(16),
        name="grams",
    )(at, *rows)


def factor_kernel(gram_ref, upper_ref, inverse_ref, work, *, block):
    experts, _, half, _ = gram_ref.shape
    size = 2 * half
    lanes = 128
    groups = lanes // block
    tiles = experts // groups
    rows_h = lax.broadcasted_iota(jnp.int32, (half, half), 0)
    cols_h = lax.broadcasted_iota(jnp.int32, (half, half), 1)
    ridge_h = jnp.where(rows_h == cols_h, RIDGE, 0.0).astype(jnp.float32)
    for e in range(experts):
        work[e, :half, :half] = gram_ref[e, 0] + ridge_h
        work[e, :half, half:] = gram_ref[e, 1]
        work[e, half:, half:] = gram_ref[e, 2] + ridge_h
    lane = lax.broadcasted_iota(jnp.int32, (block, lanes), 1)
    row = lax.broadcasted_iota(jnp.int32, (block, lanes), 0)
    unit = jnp.where(lane % block == row, 1.0, 0.0).astype(jnp.float32)
    base = (lane // block) * block
    for k in range(size // block):
        lo, hi = k * block, (k + 1) * block
        packed = [
            jnp.concatenate([work[t * groups + g, lo:hi, lo:hi] for g in range(groups)], axis=1)
            for t in range(tiles)
        ]
        inverse = [unit for _ in range(tiles)]
        scales = [jnp.ones((block, lanes), jnp.float32) for _ in range(tiles)]
        for j in range(0, block, 4):
            for t in range(tiles):
                s, n = packed[t], inverse[t]
                columns = [
                    jnp.take_along_axis(s, base + (j + i), axis=1, mode="promise_in_bounds")
                    for i in range(4)
                ]
                heads = [s[j + i : j + i + 1, :] for i in range(4)]
                tails = [n[j + i : j + i + 1, :] for i in range(4)]
                for i in range(4):
                    at = j + i
                    root = lax.rsqrt(columns[i][at : at + 1, :])
                    inv = root * root
                    scales[t] = jnp.where(row == at, root, scales[t])
                    factor = jnp.where(row > at, columns[i] * inv, 0.0)
                    for m in range(i + 1, 4):
                        ratio = columns[m][at : at + 1, :] * inv
                        columns[m] = columns[m] - columns[i] * ratio
                    s = s - factor * heads[i]
                    n = n - factor * tails[i]
                    for m in range(i + 1, 4):
                        ratio = factor[j + m : j + m + 1, :]
                        heads[m] = heads[m] - ratio * heads[i]
                        tails[m] = tails[m] - ratio * tails[i]
                packed[t], inverse[t] = s, n
        packed = [jnp.where(lane % block >= row, s * c, 0.0) for s, c in zip(packed, scales)]
        inverse = [n * c for n, c in zip(inverse, scales)]
        for e in range(experts):
            t, g = e // groups, e % groups
            work[e, lo:hi, lo:hi] = jnp.eye(block, dtype=jnp.float32)
            strip = exact_dot(
                inverse[t][:, g * block : (g + 1) * block], work[e, lo:hi, :], ((1,), (0,))
            )
            if lo:
                upper_ref[e, lo:hi, :lo] = jnp.zeros((block, lo), jnp.float32)
            upper_ref[e, lo:hi, lo:hi] = packed[t][:, g * block : (g + 1) * block]
            work[e, lo:hi, :] = strip
            if hi < size:
                upper_ref[e, lo:hi, hi:] = strip[:, hi:]
                work[e, hi:, lo:hi] = jnp.zeros((size - hi, block), jnp.float32)
                work[e, hi:, :] = work[e, hi:, :] - exact_dot(strip[:, hi:], strip, ((0,), (0,)))
    rows = lax.broadcasted_iota(jnp.int32, (size, size), 0)
    cols = lax.broadcasted_iota(jnp.int32, (size, size), 1)
    for e in range(experts):
        whole = jnp.where(rows >= cols, work[e], 0.0)
        high = whole.astype(jnp.bfloat16)
        inverse_ref[0, e] = high
        inverse_ref[1, e] = (whole - high.astype(jnp.float32)).astype(jnp.bfloat16)


def factorize(grams):
    experts, _, half, _ = grams.shape
    square = (experts, 2 * half, 2 * half)
    return pl.pallas_call(
        functools.partial(factor_kernel, block=BLOCK),
        in_specs=[WHOLE],
        out_specs=(WHOLE, WHOLE),
        out_shape=(
            jax.ShapeDtypeStruct(square, jnp.float32),
            jax.ShapeDtypeStruct((2,) + square, jnp.bfloat16),
        ),
        scratch_shapes=[pltpu.VMEM(square, jnp.float32)],
        compiler_params=params(24),
        name="factorize",
    )(grams)


def whiten_kernel(at_ref, mine_ref, other_ref, *refs, capacity):
    *row_refs, codes_ref = refs
    count = mine_ref.shape[1]
    y, x, core = at_ref[0], at_ref[1], at_ref[2]
    across = (((1,), (1,)), ((), ()))
    terms = [
        [
            jnp.where(core == e // count, mine_ref[term, e % count], other_ref[term, e % count])
            for term in range(2)
        ]
        for e in range(2 * count)
    ]
    for away, rows_ref in zip((0, 1, -1, 2), row_refs):
        found = [
            sum(
                lax.dot_general(rows_ref[e], term, across, preferred_element_type=jnp.float32)
                for term in terms[e]
            )
            for e in range(2 * count)
        ]
        for i, step in enumerate(NEAR):
            owner = lax.rem(y + step + SIDE, SIDE) * SIDE + lax.rem(x + away + SIDE, SIDE)
            own = slice(i * capacity, (i + 1) * capacity)
            codes_ref[owner] = jnp.concatenate([f[own] for f in found], axis=0).astype(
                codes_ref.dtype
            )


def whiten(at, mine, other, rows, capacity):
    _, count, size, _ = mine.shape
    return pl.pallas_call(
        functools.partial(whiten_kernel, capacity=capacity),
        in_specs=[SCALARS] + [WHOLE] * (2 + len(rows)),
        out_specs=WHOLE,
        out_shape=jax.ShapeDtypeStruct((SIDE * SIDE, 2 * count * capacity, size), jnp.bfloat16),
        compiler_params=params(24),
        name="whiten",
    )(at, mine, other, *rows)


def place_kernel(slot_ref, rows_ref, out_ref, *, width):
    tokens, top_k = slot_ref.shape
    count = tokens * top_k
    spread = jnp.broadcast_to(slot_ref[...][:, None, :], (tokens, top_k, top_k))
    lane = lax.broadcasted_iota(jnp.int32, (count, top_k), 1)
    row = lax.broadcasted_iota(jnp.int32, (count, top_k), 0)
    own = jnp.where(lane == row % top_k, spread.reshape(count, top_k), 0.0)
    slot = jnp.sum(own, axis=1, keepdims=True)
    column = lax.broadcasted_iota(jnp.int32, (count, width), 1).astype(jnp.float32)
    total = jnp.zeros(out_ref.shape, jnp.float32)
    for first in range(0, rows_ref.shape[0], width):
        pick = jnp.where(slot - float(first) == column, 1.0, 0.0).astype(rows_ref.dtype)
        total += dot(pick, rows_ref[first : first + width, :])
    out_ref[...] = total.astype(out_ref.dtype)


def place(slot, rows, step=128, width=512):
    tokens, top_k = slot.shape
    return pl.pallas_call(
        functools.partial(place_kernel, width=width),
        grid=(tokens // step,),
        in_specs=[
            pl.BlockSpec((step, top_k), lambda i: (i, 0)),
            pl.BlockSpec(rows.shape, lambda i: (0, 0)),
        ],
        out_specs=pl.BlockSpec((step * top_k, rows.shape[1]), lambda i: (i, 0)),
        out_shape=jax.ShapeDtypeStruct((tokens * top_k, rows.shape[1]), rows.dtype),
        compiler_params=params(40),
        name="place",
    )(slot, rows)


def slot_ranks(ids, first, experts):
    blocks, rows, _ = ids.shape
    wanted = first + jnp.arange(experts, dtype=jnp.int32)
    named = (jnp.swapaxes(ids, 1, 2)[:, :, None, :] == wanted[None, None, :, None]).any(axis=1)
    later = jnp.arange(rows)[:, None] < jnp.arange(rows)[None, :]
    rank = dot(named.reshape(-1, rows).astype(jnp.bfloat16), later.astype(jnp.bfloat16))
    return jnp.where(named, rank.reshape(named.shape), -1.0)


def sum_over_tok(mine, other):
    shape = mine.shape
    lanes = shape[-1]
    layers = lax.axis_size("z")
    mine = mine + shift(other, "c", 1)
    pieces = lax.all_to_all(mine.reshape(layers, -1, lanes), "z", 0, 0, tiled=True)
    return lax.all_gather(jnp.sum(pieces, axis=0), "z", tiled=True).reshape(shape)


def local(tokens, first_factor, expert_ids):
    groups = lax.axis_size(("y", "x"))
    tok_ranks = lax.axis_size(("z", "c"))
    per_group, model_dim, rank_k = first_factor.shape
    tok_rows, top_k = expert_ids.shape
    experts = groups * per_group
    capacity = tok_rows * top_k * 5 // (4 * experts)
    gram_scale = experts / (top_k * tok_rows * tok_ranks * groups)
    y, x, core = lax.axis_index("y"), lax.axis_index("x"), lax.axis_index("c")
    at = jnp.stack([y, x, core]).astype(jnp.int32)

    depth = model_dim * 5 // 8
    thin = depth // tok_ranks
    thick = (model_dim - depth) // 2
    middle = per_group // 2
    half_rows = tok_rows // 2
    tied = lax.optimization_barrier
    lanes = 128
    tagged = jnp.concatenate(
        [tokens, jnp.pad(expert_ids.astype(tokens.dtype), ((0, 0), (0, lanes - top_k)))], axis=1
    )
    slices = lax.dynamic_slice_in_dim(first_factor, lax.axis_index(("z", "c")) * thin, thin, 1)
    thick_slice = lax.dynamic_slice_in_dim(first_factor, depth + core * thick, thick, 1)
    slices_before, slices_after, slices_far = shift(slices, "x", 1), shift(slices, "x", -1), shift(slices, "x", 2)
    tagged, thick_slice, slices_before, slices_after, slices_far = tied(
        (tagged, thick_slice, slices_before, slices_after, slices_far)
    )
    shared = lax.all_gather(jnp.stack([slices_before, slices_after, slices_far]), ("z", "c"))
    mine_before, mine_after = tied((shift(thick_slice, "x", 1), shift(thick_slice, "x", -1)))
    tokens_before, tokens_after, mine_before, mine_after, other_before, other_after = tied(
        (
            shift(tagged, "y", 1),
            shift(tagged, "y", -1),
            mine_before,
            mine_after,
            shift(mine_before, "c", 1),
            shift(mine_after, "c", 1),
        )
    )
    tokens_far = [shift(tokens_before[:half_rows], "y", 1), shift(tokens_after[half_rows:], "y", -1)]
    mine_far = [shift(mine_before[:middle], "x", 1), shift(mine_after[middle:], "x", -1)]
    ids_of = lambda a: a[:, model_dim : model_dim + top_k].astype(jnp.int32)
    first_of = y * SIDE * per_group
    near_ids = jnp.stack([expert_ids, ids_of(tokens_before)])
    near = select(
        slot_ranks(near_ids, first_of, SIDE * per_group),
        tokens,
        [tokens_before],
        capacity,
        model_dim,
    )
    near, *arrived = tied((near, *tokens_far, *mine_far))
    tokens_far, mine_far = arrived[:2], arrived[2:]
    other_far = [shift(a, "c", 1) for a in mine_far]
    far_ids = jnp.stack(
        [ids_of(tokens_after), jnp.concatenate([ids_of(a) for a in tokens_far], axis=0)]
    )
    far = select(
        slot_ranks(far_ids, first_of, SIDE * per_group),
        tokens_after,
        tokens_far,
        capacity,
        model_dim,
    )
    far, *other_far = tied((far, *other_far))

    def projected(step, factors, start, count, index=None):
        where = jnp.stack([(x + step) % SIDE, core]).astype(jnp.int32)
        return project(where, near, far, factors, per_group, start, count, index)

    to_far = [
        projected(2, [shared, mine_far[i], other_far[i]], i * middle, middle, 2) for i in range(2)
    ]
    near, far, *to_far = tied((near, far, *to_far))
    from_far = [shift(shift(a, "x", way), "x", way) for a, way in zip(to_far, (1, -1))]
    to_before = projected(-1, [shared, mine_before, other_before], 0, per_group, 0)
    near, far, to_before = tied((near, far, to_before))
    from_after = shift(to_before, "x", -1)
    to_after = projected(1, [shared, mine_after, other_after], 0, per_group, 1)
    near, far, to_after = tied((near, far, to_after))
    from_before = shift(to_after, "x", 1)
    rows_own = projected(0, [first_factor], 0, per_group)
    rows_own, expert_ids = tied((rows_own, expert_ids))
    from_far = jnp.concatenate(from_far, axis=0)
    rows = [rows_own, from_after, from_before, from_far]

    upper, inverse = factorize(sum_over_tok(*partial_grams(at, rows, gram_scale)))
    codes = whiten(at, inverse, shift(inverse, "c", 1), rows, capacity)
    upper, codes = tied((upper, codes))
    returned = lax.all_to_all(codes, ("y", "x"), 0, 0, tiled=True)
    other = shift(upper, "c", 1)
    upper = jnp.where(
        core == 0, jnp.concatenate([upper, other]), jnp.concatenate([other, upper])
    )

    own_ranks = slot_ranks(expert_ids[None], 0, experts)[0]
    named = expert_ids.T[:, None, :] == jnp.arange(experts, dtype=jnp.int32)[None, :, None]
    slot = (expert_ids.T * capacity).astype(jnp.float32) + jnp.sum(
        jnp.where(named, own_ranks, 0.0), axis=1
    )
    gathered = place(slot.T, returned.reshape(experts * capacity, rank_k))
    return (gathered.reshape(tok_rows, top_k, rank_k), upper)


def solution(mesh):
    fine = Mesh(mesh.devices.reshape(-1, 2, SIDE, SIDE), ("z", "c", "y", "x"))
    every = ("z", "c", "y", "x")
    in_specs = (P(every, None), P(("y", "x"), None, None), P(every, None))
    out_specs = (P(every, None, None), P(("y", "x"), None, None))
    return jax.shard_map(local, mesh=fine, in_specs=in_specs, out_specs=out_specs, check_vma=False)
```
